256 devices in a mesh: pts: 64 (over z, y, core), out: 4 (over x).
Axes of the slice: x: 4, y: 4, z: 8, core: 2. Of those that a mesh axis runs over, the one named last changes fastest.
Arguments:
- points: bfloat16 [262144, 256], P('pts'), may hold values from -0.625 to 0.625
- rep_weights: float32 [4, 262144, 16], P('out', 'pts'), may hold values from -6 to 6
- batch_index: int32 [512], replicated, may hold values from 0 to 262143
- targets: float32 [4, 512, 16], replicated, may hold values from -6 to 6
- noise_var: float32 [4], replicated, may hold values from 0.5 to 2
- coregion: float32 [4, 4], replicated, as said below
- frequencies: bfloat16 [256, 2048], replicated, may hold values from -12 to 12
- phases: float32 [2048], replicated, may hold values from -3.140625 to 3.140625
Outputs:
- new_weights: float32 [4, 262144, 16], P('out', 'pts')
The draws below stay inside these ranges and needn't reach their ends.
Inputs may be any that keep to these rules, and one draw needn't show every extreme that they name: `coregion`: symmetric and positive definite.
All inputs are finite; a program needn't handle non-finite values.
Results may differ from the reference program's by a relative error of at most 0.0031.
Values may be sent and summed in bfloat16 or wider, within the bound.
No kernel may reach another device: no remote copies, remote signals or barrier semaphores. Data moves between devices by JAX's collectives and lax.ppermute only.
A program may use at most 128 MiB of HBM per device.

```python
import math
import jax
import jax.numpy as jnp
from jax import lax

E = 256
F = 2048
S = 16
N_DEV = 4096
M = 512
P_SIZE = 4
N = 262144


def draw_coregion(key, part):
    key = jax.random.fold_in(key, 11)
    first_key, second_key = jax.random.split(key)
    factor = jax.random.normal(first_key, (P_SIZE, P_SIZE), jnp.float32)
    diagonal = jax.random.uniform(second_key, (P_SIZE,), jnp.float32, 0.5, 1.5)
    outer = jnp.sum(factor[:, None, :] * factor[None, :, :], axis=2) / P_SIZE
    return (jnp.diag(diagonal) + outer) * (25.0 * float(N) ** (-0.5))


def plant(values, own_key, low, top_value):
    shape = values.shape
    spot = [jax.random.randint(jax.random.fold_in(own_key, axis), (), 0, shape[axis]) for axis in range(len(shape))]
    values = values.at[tuple(spot)].set(low)
    longest = shape.index(max(shape))
    spot[longest] = (spot[longest] + 1) % shape[longest]
    return values.at[tuple(spot)].set(top_value)


def block_levels(key, extent, shards, low, top_value):
    gain, own = 1.0, jax.random.fold_in(key, 6)
    for axis_at, parts in shards:
        heights = jnp.exp(jax.random.uniform(jax.random.fold_in(own, axis_at), (parts,), jnp.float32, low / len(shards), top_value / len(shards)))
        gain = gain * jnp.repeat(heights, extent[axis_at] // parts).reshape([-1 if axis == axis_at else 1 for axis in range(len(extent))])
    return gain


def normal_values(stream_key, dims, width, most, cuts=(), dtype=jnp.bfloat16):
    loudness = block_levels(stream_key, dims, cuts, -0.22, 0.18) if cuts else 1.0
    array = jax.random.normal(stream_key, dims, jnp.float32) * width * loudness
    return jnp.minimum(jnp.maximum(array, -most), most).astype(dtype)


def setup_inputs(seed: int = 0) -> dict:
    keys = jax.random.split(jax.random.key(seed), 9)
    return {
        "points": normal_values(keys[0], (N, E), (1.75 * E ** -0.5), 0.625, ((0, 64),)),
        "rep_weights": normal_values(keys[1], (P_SIZE, N, S), 1.0, 6.0, ((0, 4), (1, 64)), jnp.float32),
        "batch_index": plant(jax.random.randint(keys[2], (M,), 0, N), jax.random.fold_in(keys[2], 1), 0, N - 1).astype(jnp.int32),
        "targets": normal_values(keys[3], (P_SIZE, M, S), 1.0, 6.0, (), jnp.float32),
        "noise_var": jnp.clip(jnp.exp(jax.random.uniform(keys[4], (P_SIZE,), jnp.float32, math.log(0.5), math.log(2.0))), 0.5, 2.0),
        "coregion": draw_coregion(jax.random.fold_in(keys[8], 71), 0),
        "frequencies": normal_values(keys[6], (E, F), 2.0, 12.0),
        "phases": jnp.clip(jax.random.uniform(keys[7], (F,), jnp.float32, -3.140625, 3.140625), -3.140625, 3.140625),
    }


LENGTH = 0.5
STEP_SIZE = 0.5

def kernel_block(batch_rows, slab):
    row_norm = lax.optimization_barrier(jnp.sum(jnp.square(batch_rows.astype(jnp.float32)), 1))
    col_norm = lax.optimization_barrier(jnp.sum(jnp.square(slab.astype(jnp.float32)), 1))
    inner = jnp.dot(batch_rows, slab.T, preferred_element_type=jnp.float32)
    squared = row_norm[:, None] + col_norm[None, :] - 2.0 * inner
    scaled_r = math.sqrt(5.0) / LENGTH * jnp.sqrt(jnp.maximum(squared, 0.0))
    return ((1.0 + scaled_r + scaled_r * scaled_r / 3.0) * jnp.exp(-scaled_r)).astype(jnp.bfloat16)

def feature_map(slab, frequencies, phases):
    angle_arg = jnp.dot(slab, frequencies, preferred_element_type=jnp.float32) + phases
    return (math.sqrt(2.0 / F) * jnp.cos(angle_arg)).astype(jnp.bfloat16)

def reference(points, rep_weights, batch_index, targets, noise_var, coregion, frequencies, phases):
    highest = lax.Precision.HIGHEST
    batch_rows = points[batch_index]
    low_weights = rep_weights.astype(jnp.bfloat16)
    nblocks = N // N_DEV
    slabs = points.reshape(nblocks, N_DEV, E)
    low_slabs = low_weights.reshape(P_SIZE, nblocks, N_DEV, S).transpose(1, 0, 2, 3)

    def first(totals, inputs):
        slab, weights = inputs
        kern = kernel_block(batch_rows, slab)
        feats = feature_map(slab, frequencies, phases)
        partial_value = totals[0] + jnp.einsum('mn,pns->pms', kern.astype(jnp.float32), weights.astype(jnp.float32))
        projected = totals[1] + jnp.einsum('nf,pns->pfs', feats.astype(jnp.float32), weights.astype(jnp.float32))
        return ((partial_value, projected), (kern, feats))
    init = (jnp.zeros((P_SIZE, M, S), jnp.float32), jnp.zeros((P_SIZE, F, S), jnp.float32))
    (partial_value, projected), (kerns, feats_all) = lax.scan(first, init, (slabs, low_slabs))
    fitted = jnp.einsum('pq,qms->pms', coregion, partial_value, precision=highest)
    scaled = (fitted - targets) / noise_var[:, None, None]
    weighted = jnp.einsum('pq,qms->pms', coregion, scaled, precision=highest).astype(jnp.bfloat16)
    mixed = jnp.einsum('pq,qfs->pfs', coregion, projected, precision=highest).astype(jnp.bfloat16)
    ratio = jnp.float32(N) / jnp.float32(M)

    def second(inputs):
        kern, feats = inputs
        data_grad = jnp.einsum('mn,pms->pns', kern.astype(jnp.float32), weighted.astype(jnp.float32))
        regular = jnp.einsum('nf,pfs->pns', feats.astype(jnp.float32), mixed.astype(jnp.float32))
        return ratio * data_grad + regular
    gradient = lax.map(second, (kerns, feats_all))
    gradient = gradient.transpose(1, 0, 2, 3).reshape(P_SIZE, N, S)
    return rep_weights - STEP_SIZE * gradient
```

```python
import math

import jax
import jax.numpy as jnp
from jax import lax
from jax.sharding import Mesh
from jax.sharding import PartitionSpec as P

LENGTH = 0.5
STEP_SIZE = 0.5
SLOTS = 8
SIN_TURNS = (
    6.283185160088695,
    -41.34165503124932,
    81.60100406363227,
    -76.54978208799582,
    39.53670460277009,
)
POINT_AXES = ("z", "y", "core")
CHIP_AXES = ("z", "y")


def cos_turns(turns):
    rest = turns - jnp.round(turns)
    quarter = 0.25 - jnp.abs(rest)
    square = quarter * quarter
    poly = jnp.float32(SIN_TURNS[-1])
    for coefficient in SIN_TURNS[-2::-1]:
        poly = poly * square + jnp.float32(coefficient)
    return poly * quarter


def matern(squared):
    scaled_square = (5.0 / (LENGTH * LENGTH)) * jnp.maximum(squared, 0.0)
    scaled_r = scaled_square * lax.rsqrt(jnp.maximum(scaled_square, 1e-30))
    return ((1.0 + scaled_r + scaled_square * (1.0 / 3.0)) * jnp.exp(-scaled_r)).astype(jnp.bfloat16)


def swap_core(value):
    return lax.ppermute(value, "core", [(0, 1), (1, 0)])


def shards(points, rep_weights, batch_index, targets, noise_var, coregion, frequencies, phases):
    highest = lax.Precision.HIGHEST
    n_out = lax.axis_size("out")
    n_chips = lax.axis_size("z") * lax.axis_size("y")
    n_pts = 2 * n_chips
    rows, width = points.shape
    draws = rep_weights.shape[2]
    minibatch = batch_index.shape[0]
    total_features = frequencies.shape[1]
    own_rows = minibatch // n_out
    own_features = total_features // n_out
    out = lax.axis_index("out")
    core = lax.axis_index("core")
    chip = lax.axis_index("z") * lax.axis_size("y") + lax.axis_index("y")
    shard = chip * 2 + core
    ratio = (rows * n_pts) / minibatch

    m_iota = lax.iota(jnp.int32, minibatch)
    before = (batch_index[None, :] < batch_index[:, None]) | (
        (batch_index[None, :] == batch_index[:, None]) & (m_iota[None, :] < m_iota[:, None])
    )
    rank = jnp.sum(before.astype(jnp.int32), 1)
    own_rank = lax.iota(jnp.int32, own_rows) * n_out + out
    chosen = own_rank[:, None] == rank[None, :]
    own_index = jnp.sum(jnp.where(chosen, batch_index[None, :], 0), 1)
    own_shard = own_index // rows
    starts = jnp.sum((own_index[None, :] < (own_shard * rows)[:, None]).astype(jnp.int32), 1)
    slot = lax.iota(jnp.int32, own_rows) - starts
    same_shard = (batch_index // rows)[None, :] == (batch_index // rows)[:, None]
    most = jnp.max(jnp.sum(same_shard.astype(jnp.int32), 1))
    overflow = most > SLOTS * n_out

    local = jnp.pad(own_index - shard * rows, (0, SLOTS))
    first = jnp.sum((own_index < shard * rows).astype(jnp.int32))
    mine = jnp.clip(lax.dynamic_slice(local, (first,), (SLOTS,)), 0, rows - 1)
    sent_rows = points[mine].reshape(SLOTS, 2, width // 2).transpose(1, 0, 2).reshape(2 * SLOTS, width // 2)
    sent_rows = jnp.broadcast_to(sent_rows[None], (n_chips, 2 * SLOTS, width // 2))
    got_rows = lax.all_to_all(sent_rows, CHIP_AXES, 0, 0)

    own_weights = rep_weights[0].T
    low = own_weights.astype(jnp.bfloat16)
    all_low = [low]
    for k in range(1, n_out):
        all_low.append(lax.ppermute(low, "out", [(i, (i + k) % n_out) for i in range(n_out)]))

    freq = lax.dynamic_slice(frequencies, (0, out * own_features), (width, own_features))
    phase = lax.dynamic_slice(phases, (out * own_features,), (own_features,))
    turns = lax.dot_general(
        freq, points, (((0,), (1,)), ((), ())), preferred_element_type=jnp.float32
    ) * (0.5 / math.pi) + (phase * (0.5 / math.pi))[:, None]
    feats = (math.sqrt(2.0 / total_features) * cos_turns(turns)).astype(jnp.bfloat16)

    weights = jnp.concatenate(all_low, 0)
    projected = lax.dot_general(
        weights, feats, (((1,), (1,)), ((), ())), preferred_element_type=jnp.float32
    )
    cols = n_out * draws
    tiles = projected.reshape(cols // 8, 8, own_features // 128, 128).transpose(0, 2, 1, 3)
    tiles = tiles.reshape(n_chips, 8, 128)
    got = jnp.sum(lax.all_to_all(tiles, CHIP_AXES, 0, 0), 0)
    got = got + swap_core(got)
    got = lax.all_to_all(jnp.broadcast_to(got[None], (n_chips, 8, 128)), CHIP_AXES, 0, 0)
    projected = got.reshape(cols // 8, own_features // 128, 8, 128).transpose(0, 2, 1, 3)
    projected = projected.reshape(n_out, draws * own_features)

    other_rows = swap_core(got_rows)

    def place(_):
        own_core = (own_shard % 2) == core
        at = (own_shard // 2) * (2 * SLOTS) + slot
        columns = lax.iota(jnp.int32, n_chips * 2 * SLOTS)
        halves = []
        for half in range(2):
            part = 0.0
            for source, held in ((own_core, got_rows), (~own_core, other_rows)):
                pick = ((at + half * SLOTS)[:, None] == columns[None, :]) & source[:, None]
                part = part + jnp.dot(
                    pick.astype(jnp.bfloat16),
                    held.reshape(n_chips * 2 * SLOTS, width // 2),
                    preferred_element_type=jnp.float32,
                )
            halves.append(part)
        return jnp.concatenate(halves, 1).astype(jnp.bfloat16)

    def fetch(_):
        at = own_index - shard * rows
        inside = (at >= 0) & (at < rows)
        picked = jnp.where(inside[:, None], points[jnp.clip(at, 0, rows - 1)].astype(jnp.float32), 0.0)
        return lax.psum(picked, POINT_AXES).astype(jnp.bfloat16)

    batch_rows = lax.cond(overflow, fetch, place, 0)

    row_norm = jnp.sum(jnp.square(batch_rows.astype(jnp.float32)), 1)
    col_norm = jnp.sum(jnp.square(points.astype(jnp.float32)), 1)
    inner = lax.dot_general(
        batch_rows, points, (((1,), (1,)), ((), ())), preferred_element_type=jnp.float32
    )
    kern = matern(row_norm[:, None] + col_norm[None, :] - 2.0 * inner)
    partial = lax.dot_general(
        weights, kern, (((1,), (1,)), ((), ())), preferred_element_type=jnp.float32
    )
    half_cols = cols // 2
    halves = partial.reshape(2, half_cols, own_rows)
    kept = lax.dynamic_index_in_dim(halves, core, 0, keepdims=False)
    given = lax.dynamic_index_in_dim(halves, 1 - core, 0, keepdims=False)
    kept = (kept + swap_core(given)).astype(jnp.bfloat16)
    kept = lax.all_to_all(jnp.broadcast_to(kept[None], (n_chips, half_cols, own_rows)), CHIP_AXES, 0, 0)
    kept = jnp.sum(kept.astype(jnp.float32), 0)
    other = swap_core(kept)
    lower = jnp.where(core == 0, kept, other)
    upper = jnp.where(core == 0, other, kept)
    partial = jnp.concatenate([lower, upper], 0).reshape(n_out, draws * own_rows)

    order = (out - lax.iota(jnp.int32, n_out)) % n_out
    mixer = coregion[order][:, order]
    noise = noise_var[order]
    own_targets = jnp.einsum("im,qms->qsi", chosen.astype(jnp.float32), targets[order], precision=highest)
    fitted = jnp.dot(mixer, partial, precision=highest)
    scaled = (fitted - own_targets.reshape(n_out, draws * own_rows)) / noise[:, None]
    weighted = jnp.dot(mixer, scaled, precision=highest).astype(jnp.bfloat16)
    mixed = jnp.dot(mixer, projected, precision=highest).astype(jnp.bfloat16)
    gradient = ratio * jnp.dot(
        weighted.reshape(cols, own_rows), kern, preferred_element_type=jnp.float32
    ) + jnp.dot(mixed.reshape(cols, own_features), feats, preferred_element_type=jnp.float32)
    gradient = gradient.reshape(n_out, draws, rows)
    total = gradient[0]
    sent = gradient[1:].astype(jnp.bfloat16)
    for k in range(1, n_out):
        part = lax.ppermute(sent[k - 1], "out", [(i, (i - k) % n_out) for i in range(n_out)])
        total = total + part.astype(jnp.float32)
    return (own_weights - STEP_SIZE * total).T[None]


def solution(mesh):
    fine = Mesh(mesh.devices.reshape(8, 4, 2, 4), ("z", "y", "core", "out"))
    in_specs = (P(POINT_AXES, None), P("out", POINT_AXES, None), P(), P(), P(), P(), P(), P())
    out_specs = P("out", POINT_AXES, None)
    return jax.shard_map(shards, mesh=fine, in_specs=in_specs, out_specs=out_specs, check_vma=False)
```

```python
import math

import jax
import jax.numpy as jnp
from jax import lax
from jax.sharding import Mesh
from jax.sharding import PartitionSpec as P

LENGTH = 0.5
STEP_SIZE = 0.5
SLOTS = 8
SIN_TURNS = (
    6.283185160088695,
    -41.34165503124932,
    81.60100406363227,
    -76.54978208799582,
    39.53670460277009,
)
POINT_AXES = ("z", "y", "core")
CHIP_AXES = ("z", "y")


def cos_turns(turns):
    rest = turns - jnp.round(turns)
    quarter = 0.25 - jnp.abs(rest)
    square = quarter * quarter
    poly = jnp.float32(SIN_TURNS[-1])
    for coefficient in SIN_TURNS[-2::-1]:
        poly = poly * square + jnp.float32(coefficient)
    return poly * quarter


def matern(squared):
    scaled_square = (5.0 / (LENGTH * LENGTH)) * jnp.maximum(squared, 0.0)
    scaled_r = scaled_square * lax.rsqrt(jnp.maximum(scaled_square, 1e-30))
    return ((1.0 + scaled_r + scaled_square * (1.0 / 3.0)) * jnp.exp(-scaled_r)).astype(jnp.bfloat16)


def swap_core(value):
    return lax.ppermute(value, "core", [(0, 1), (1, 0)])


def shards(points, rep_weights, batch_index, targets, noise_var, coregion, frequencies, phases):
    highest = lax.Precision.HIGHEST
    n_out = lax.axis_size("out")
    n_chips = lax.axis_size("z") * lax.axis_size("y")
    n_pts = 2 * n_chips
    rows, width = points.shape
    draws = rep_weights.shape[2]
    minibatch = batch_index.shape[0]
    total_features = frequencies.shape[1]
    own_rows = minibatch // n_out
    own_features = total_features // n_out
    out = lax.axis_index("out")
    core = lax.axis_index("core")
    chip = lax.axis_index("z") * lax.axis_size("y") + lax.axis_index("y")
    shard = chip * 2 + core
    ratio = (rows * n_pts) / minibatch

    m_iota = lax.iota(jnp.int32, minibatch)
    before = (batch_index[None, :] < batch_index[:, None]) | (
        (batch_index[None, :] == batch_index[:, None]) & (m_iota[None, :] < m_iota[:, None])
    )
    rank = jnp.sum(before.astype(jnp.int32), 1)
    own_rank = lax.iota(jnp.int32, own_rows) * n_out + out
    chosen = own_rank[:, None] == rank[None, :]
    own_index = jnp.sum(jnp.where(chosen, batch_index[None, :], 0), 1)
    own_shard = own_index // rows
    starts = jnp.sum((own_index[None, :] < (own_shard * rows)[:, None]).astype(jnp.int32), 1)
    slot = lax.iota(jnp.int32, own_rows) - starts
    same_shard = (batch_index // rows)[None, :] == (batch_index // rows)[:, None]
    most = jnp.max(jnp.sum(same_shard.astype(jnp.int32), 1))
    overflow = most > SLOTS * n_out

    local = jnp.pad(own_index - shard * rows, (0, SLOTS))
    first = jnp.sum((own_index < shard * rows).astype(jnp.int32))
    mine = jnp.clip(lax.dynamic_slice(local, (first,), (SLOTS,)), 0, rows - 1)
    sent_rows = points[mine].reshape(SLOTS, 2, width // 2).transpose(1, 0, 2).reshape(2 * SLOTS, width // 2)
    sent_rows = jnp.broadcast_to(sent_rows[None], (n_chips, 2 * SLOTS, width // 2))

    own_weights = rep_weights[0].T
    low = own_weights.astype(jnp.bfloat16)
    all_low = [low]
    for k in range(1, n_out):
        all_low.append(lax.ppermute(low, "out", [(i, (i + k) % n_out) for i in range(n_out)]))

    freq = lax.dynamic_slice(frequencies, (0, out * own_features), (width, own_features))
    phase = lax.dynamic_slice(phases, (out * own_features,), (own_features,))
    turns = lax.dot_general(
        freq, points, (((0,), (1,)), ((), ())), preferred_element_type=jnp.float32
    ) * (0.5 / math.pi) + (phase * (0.5 / math.pi))[:, None]
    feats = (math.sqrt(2.0 / total_features) * cos_turns(turns)).astype(jnp.bfloat16)

    weights = jnp.concatenate(all_low, 0)
    projected = lax.dot_general(
        weights, feats, (((1,), (1,)), ((), ())), preferred_element_type=jnp.float32
    )
    cols = n_out * draws
    tiles = projected.reshape(cols // 8, 8, own_features // 128, 128).transpose(0, 2, 1, 3)
    tiles = tiles.reshape(n_chips, 8, 128)
    got = lax.all_to_all(
        jnp.concatenate([sent_rows, tiles.astype(jnp.bfloat16)], 1), CHIP_AXES, 0, 0
    )
    got_rows = got[:, : 2 * SLOTS]
    projected = jnp.sum(got[:, 2 * SLOTS :].astype(jnp.float32), 0)
    projected = (projected + swap_core(projected)).astype(jnp.bfloat16)

    other_rows = swap_core(got_rows)

    def place(_):
        own_core = (own_shard % 2) == core
        at = (own_shard // 2) * (2 * SLOTS) + slot
        columns = lax.iota(jnp.int32, n_chips * 2 * SLOTS)
        halves = []
        for half in range(2):
            part = 0.0
            for source, held in ((own_core, got_rows), (~own_core, other_rows)):
                pick = ((at + half * SLOTS)[:, None] == columns[None, :]) & source[:, None]
                part = part + jnp.dot(
                    pick.astype(jnp.bfloat16),
                    held.reshape(n_chips * 2 * SLOTS, width // 2),
                    preferred_element_type=jnp.float32,
                )
            halves.append(part)
        return jnp.concatenate(halves, 1).astype(jnp.bfloat16)

    def fetch(_):
        at = own_index - shard * rows
        inside = (at >= 0) & (at < rows)
        picked = jnp.where(inside[:, None], points[jnp.clip(at, 0, rows - 1)].astype(jnp.float32), 0.0)
        return lax.psum(picked, POINT_AXES).astype(jnp.bfloat16)

    batch_rows = lax.cond(overflow, fetch, place, 0)

    row_norm = jnp.sum(jnp.square(batch_rows.astype(jnp.float32)), 1)
    col_norm = jnp.sum(jnp.square(points.astype(jnp.float32)), 1)
    inner = lax.dot_general(
        batch_rows, points, (((1,), (1,)), ((), ())), preferred_element_type=jnp.float32
    )
    kern = matern(row_norm[:, None] + col_norm[None, :] - 2.0 * inner)
    partial = lax.dot_general(
        weights, kern, (((1,), (1,)), ((), ())), preferred_element_type=jnp.float32
    )
    half_cols = cols // 2
    halves = partial.reshape(2, half_cols, own_rows)
    kept = lax.dynamic_index_in_dim(halves, core, 0, keepdims=False)
    given = lax.dynamic_index_in_dim(halves, 1 - core, 0, keepdims=False)
    kept = (kept + swap_core(given)).astype(jnp.bfloat16)
    sent = jnp.concatenate([kept, projected], 0)
    got = lax.all_to_all(jnp.broadcast_to(sent[None], (n_chips, *sent.shape)), CHIP_AXES, 0, 0)
    projected = got[:, half_cols:].astype(jnp.float32)
    projected = projected.reshape(cols // 8, own_features // 128, 8, 128).transpose(0, 2, 1, 3)
    projected = projected.reshape(n_out, draws * own_features)
    kept = jnp.sum(got[:, :half_cols].astype(jnp.float32), 0)
    other = swap_core(kept)
    lower = jnp.where(core == 0, kept, other)
    upper = jnp.where(core == 0, other, kept)
    partial = jnp.concatenate([lower, upper], 0).reshape(n_out, draws * own_rows)

    order = (out - lax.iota(jnp.int32, n_out)) % n_out
    mixer = coregion[order][:, order]
    noise = noise_var[order]
    own_targets = jnp.einsum("im,qms->qsi", chosen.astype(jnp.float32), targets[order], precision=highest)
    fitted = jnp.dot(mixer, partial, precision=highest)
    scaled = (fitted - own_targets.reshape(n_out, draws * own_rows)) / noise[:, None]
    weighted = jnp.dot(mixer, scaled, precision=highest).astype(jnp.bfloat16)
    mixed = jnp.dot(mixer, projected, precision=highest).astype(jnp.bfloat16)
    gradient = ratio * jnp.dot(
        weighted.reshape(cols, own_rows), kern, preferred_element_type=jnp.float32
    ) + jnp.dot(mixed.reshape(cols, own_features), feats, preferred_element_type=jnp.float32)
    gradient = gradient.reshape(n_out, draws, rows)
    total = gradient[0]
    sent = gradient[1:].astype(jnp.bfloat16)
    for k in range(1, n_out):
        part = lax.ppermute(sent[k - 1], "out", [(i, (i - k) % n_out) for i in range(n_out)])
        total = total + part.astype(jnp.float32)
    return (own_weights - STEP_SIZE * total).T[None]


def solution(mesh):
    fine = Mesh(mesh.devices.reshape(8, 4, 2, 4), ("z", "y", "core", "out"))
    in_specs = (P(POINT_AXES, None), P("out", POINT_AXES, None), P(), P(), P(), P(), P(), P())
    out_specs = P("out", POINT_AXES, None)
    return jax.shard_map(shards, mesh=fine, in_specs=in_specs, out_specs=out_specs, check_vma=False)
```

```python
import functools
import math

import jax
import jax.numpy as jnp
from jax import lax
from jax.experimental import pallas as pl
from jax.experimental.pallas import tpu as pltpu
from jax.sharding import Mesh
from jax.sharding import PartitionSpec as P

LENGTH = 0.5
STEP_SIZE = 0.5
SLOTS = 8
BLOCK = 512
SIN_TURNS = (
    6.283185160088695,
    -41.34165503124932,
    81.60100406363227,
    -76.54978208799582,
    39.53670460277009,
)
POINT_AXES = ("z", "y", "core")
CHIP_AXES = ("z", "y")
BF16 = jnp.bfloat16
F32 = jnp.float32
NT = (((1,), (1,)), ((), ()))


def dot(a, b):
    return jnp.dot(a, b, preferred_element_type=F32)


def dot_nt(a, b):
    return lax.dot_general(a, b, NT, preferred_element_type=F32)


def cos_turns(turns, scale):
    rest = turns - jnp.round(turns)
    quarter = 0.25 - jnp.abs(rest)
    square = quarter * quarter
    poly = F32(SIN_TURNS[-1] * scale)
    for coefficient in SIN_TURNS[-2::-1]:
        poly = poly * square + F32(coefficient * scale)
    return poly * quarter


def split(value):
    high = value.astype(BF16)
    return high, (value - high.astype(F32)).astype(BF16)


def place_of_device():
    chip = lax.axis_index("z") * lax.axis_size("y") + lax.axis_index("y")
    return lax.axis_index("out"), lax.axis_index("core"), chip


def whole(shape):
    return pl.BlockSpec(shape, lambda i: (0,) * len(shape))


def features_kernel(index_ref, points_ref, freq_ref, phase_ref, feats_ref, sent_ref, local_ref, rows_ref):
    step = pl.program_id(0)
    out, core, chip = place_of_device()
    block = points_ref.shape[0]
    own = feats_ref.shape[1]
    n_out = freq_ref.shape[1] // own
    shard_rows = block * pl.num_programs(0)
    minibatch = index_ref.shape[1]

    @pl.when(step == 0)
    def _():
        base = (chip * 2 + core) * shard_rows
        index = index_ref[...]
        key = index * minibatch + lax.broadcasted_iota(jnp.int32, index.shape, 1)
        key_column = jnp.transpose(jnp.broadcast_to(key, (8, minibatch)))[:, :1]
        rank = jnp.sum((key_column < key).astype(jnp.int32), 0, keepdims=True)
        before = jnp.sum((index < base).astype(jnp.int32), 1, keepdims=True)
        first = (before - out + (n_out - 1)) // n_out
        inside = (index >= base) & (index < base + shard_rows) & (lax.rem(rank - out + n_out, n_out) == 0)
        slot = jnp.where(inside, (rank - out) // n_out - first, -1)
        here = slot == lax.broadcasted_iota(jnp.int32, (2 * SLOTS, minibatch), 0)
        local = jnp.sum(jnp.where(here, index - base + 1, 0), 1, keepdims=True) - 1
        local_ref[...] = jnp.broadcast_to(local, local_ref.shape)
        rows_ref[...] = jnp.zeros_like(rows_ref)

    points = points_ref[...]
    at = pl.multiple_of(out * own, own)
    phase = phase_ref[:, pl.ds(at, own)] * (0.5 / math.pi)
    turns = dot(points, freq_ref[:, pl.ds(at, own)]) * (0.5 / math.pi) + phase
    feats_ref[...] = cos_turns(turns, math.sqrt(2.0 / freq_ref.shape[1])).astype(BF16)
    pick = local_ref[:, :1] - step * block == lax.broadcasted_iota(jnp.int32, (2 * SLOTS, block), 1)
    rows_ref[...] += dot(pick.astype(F32).astype(BF16), points)

    @pl.when(step == pl.num_programs(0) - 1)
    def _():
        half = rows_ref.shape[1] // 2
        rows = rows_ref[...]
        sent_ref[...] = jnp.concatenate([rows[:SLOTS, :half], rows[:SLOTS, half:]], 0).astype(BF16)


def project_kernel(n_out, *refs):
    weight_refs, (feats_ref, sent_ref, pack_ref, sum_ref) = refs[:n_out], refs[n_out:]
    step = pl.program_id(0)

    @pl.when(step == 0)
    def _():
        sum_ref[...] = jnp.zeros_like(sum_ref)

    weights = jnp.concatenate([ref[...] for ref in weight_refs], 0)
    sum_ref[...] += dot(weights, feats_ref[...])

    @pl.when(step == pl.num_programs(0) - 1)
    def _():
        across = sum_ref.shape[1] // 128
        for at in range(pack_ref.shape[0]):
            r, c = divmod(at, across)
            high, low = split(sum_ref[8 * r : 8 * r + 8, 128 * c : 128 * c + 128])
            pack_ref[at, :16] = sent_ref[...]
            pack_ref[at, 16:] = jnp.concatenate([high.astype(F32), low.astype(F32)], 0).astype(BF16)


def gram_kernel(n_out, direct, *refs):
    weight_refs = refs[:n_out]
    at_ref, own_ref, other_ref, points_ref, norm_ref = refs[n_out : n_out + 5]
    kern_ref, kept_ref, given_ref, tile_ref, rows_ref, row_norm_ref, sum_ref = refs[n_out + 5 :]
    step = pl.program_id(0)

    @pl.when(step == 0)
    def _():
        peers, height, lanes = own_ref.shape
        if direct:
            rows = at_ref[...].astype(F32)
        else:
            columns = lax.broadcasted_iota(jnp.int32, (rows_ref.shape[0], peers * height), 1)
            halves = []
            for half in range(2):
                part = 0.0
                for source, held in enumerate((own_ref, other_ref)):
                    pick = (at_ref[source][:, :1] + half * SLOTS == columns).astype(F32).astype(BF16)
                    part = part + dot(pick, held[...].reshape(peers * height, lanes))
                halves.append(part)
            rows = jnp.concatenate(halves, 1)
        rows_ref[...] = rows.astype(BF16)
        row_norm_ref[...] = jnp.broadcast_to(jnp.sum(rows * rows, 1, keepdims=True), row_norm_ref.shape)
        sum_ref[...] = jnp.zeros_like(sum_ref)
        tile = jnp.sum(own_ref[:, 16:].astype(F32), 0) + jnp.sum(other_ref[:, 16:].astype(F32), 0)
        tile_ref[...] = tile[:8] + tile[8:]

    inner = dot_nt(rows_ref[...], points_ref[...])
    squared = row_norm_ref[:, :1] + norm_ref[...] - 2.0 * inner
    scaled_square = (5.0 / (LENGTH * LENGTH)) * jnp.maximum(squared, 0.0)
    scaled_r = scaled_square * lax.rsqrt(jnp.maximum(scaled_square, 1e-30))
    kern = (1.0 + scaled_r + scaled_square * (1.0 / 3.0)) * jnp.exp(-scaled_r)
    kern = kern.astype(BF16)
    kern_ref[...] = kern
    weights = jnp.concatenate([ref[...] for ref in weight_refs], 0)
    sum_ref[...] += dot_nt(weights, kern)

    @pl.when(step == pl.num_programs(0) - 1)
    def _():
        half = kept_ref.shape[0]
        core = lax.axis_index("core")
        lower, upper = sum_ref[:half], sum_ref[half:]
        kept_ref[...] = jnp.where(core == 0, lower, upper)
        given_ref[...] = jnp.where(core == 0, upper, lower)


def pack_kernel(kept_ref, came_ref, tile_ref, pack_ref):
    half = kept_ref.shape[0]
    high, low = split(tile_ref[...])
    value = jnp.concatenate([kept_ref[...] + came_ref[...], high.astype(F32), low.astype(F32)], 0).astype(BF16)
    pack_ref[...] = jnp.broadcast_to(value[None], pack_ref.shape)


def step_kernel(n_out, ratio, *refs):
    coregion_ref, noise_ref, targets_ref, own_ref, other_ref, feats_ref, kern_ref, rep_ref = refs[:8]
    base_ref, part_refs, (mixed_ref, weighted_ref) = refs[8], refs[9 : 8 + n_out], refs[8 + n_out :]
    draws = rep_ref.shape[0]
    half = n_out * draws // 2

    @pl.when(pl.program_id(0) == 0)
    def _():
        out, core, _ = place_of_device()
        order = [lax.rem(out - k + n_out, n_out) for k in range(n_out)]
        mixer = [[coregion_ref[a, b] for b in order] for a in order]

        def mix(values):
            return [sum(c * v for c, v in zip(line, values)) for line in mixer]

        own = jnp.sum(own_ref[:, :half].astype(F32), 0)
        other = jnp.sum(other_ref[:, :half].astype(F32), 0)
        total = jnp.concatenate([jnp.where(core == 0, own, other), jnp.where(core == 0, other, own)], 0)
        fitted = mix([total[draws * k : draws * (k + 1)] for k in range(n_out)])
        scaled = [
            (fitted[k] - targets_ref[draws * k : draws * (k + 1)]) / noise_ref[order[k]] for k in range(n_out)
        ]
        weighted = jnp.concatenate(mix(scaled), 0).astype(BF16)
        weighted_ref[...] = (weighted.astype(F32) * ratio).astype(BF16)
        across = mixed_ref.shape[1] // 128
        tiles = [own_ref[p, half:].astype(F32) for p in range(own_ref.shape[0])]
        tiles = [tile[:8] + tile[8:] for tile in tiles]
        lines = [
            jnp.concatenate(tiles[across * r : across * (r + 1)], 1) for r in range(n_out * draws // 8)
        ]
        each = draws // 8
        projected = [jnp.concatenate(lines[each * k : each * (k + 1)], 0) for k in range(n_out)]
        mixed_ref[...] = jnp.concatenate(mix(projected), 0).astype(BF16)

    gradient = dot(weighted_ref[...], kern_ref[...]) + dot_nt(mixed_ref[...], feats_ref[...])
    change = -STEP_SIZE * gradient
    base_ref[...] = rep_ref[...] + change[:draws]
    for k, ref in enumerate(part_refs, 1):
        ref[...] = change[draws * k : draws * (k + 1)].astype(BF16)


def swap_core(value):
    return lax.ppermute(value, "core", [(0, 1), (1, 0)])


def params():
    return pltpu.CompilerParams(dimension_semantics=("arbitrary",), vmem_limit_bytes=32 * 1024 * 1024)


def shards(points, rep_weights, batch_index, targets, noise_var, coregion, frequencies, phases):
    highest = lax.Precision.HIGHEST
    n_out = lax.axis_size("out")
    n_chips = lax.axis_size("z") * lax.axis_size("y")
    n_pts = 2 * n_chips
    rows, width = points.shape
    draws = rep_weights.shape[2]
    minibatch = batch_index.shape[0]
    own_rows = minibatch // n_out
    own_features = frequencies.shape[1] // n_out
    cols = n_out * draws
    steps = rows // BLOCK
    out, core, chip = place_of_device()
    shard = chip * 2 + core
    ratio = (rows * n_pts) / minibatch

    own_weights = rep_weights[0].T
    low = own_weights.astype(BF16)
    weights = [low]
    for k in range(1, n_out):
        weights.append(lax.ppermute(low, "out", [(i, (i + k) % n_out) for i in range(n_out)]))
    weight_specs = [pl.BlockSpec((draws, BLOCK), lambda i: (0, i))] * n_out
    point_spec = pl.BlockSpec((BLOCK, width), lambda i: (i, 0))
    feat_spec = pl.BlockSpec((BLOCK, own_features), lambda i: (i, 0))
    kern_spec = pl.BlockSpec((own_rows, BLOCK), lambda i: (0, i))
    draw_spec = pl.BlockSpec((draws, BLOCK), lambda i: (0, i))

    feats, sent_rows = pl.pallas_call(
        features_kernel,
        grid=(steps,),
        out_shape=(
            jax.ShapeDtypeStruct((rows, own_features), BF16),
            jax.ShapeDtypeStruct((2 * SLOTS, width // 2), BF16),
        ),
        in_specs=[
            whole((1, minibatch)),
            point_spec,
            whole(frequencies.shape),
            whole((1, phases.shape[0])),
        ],
        out_specs=(feat_spec, whole((2 * SLOTS, width // 2))),
        scratch_shapes=[pltpu.VMEM((2 * SLOTS, 128), jnp.int32), pltpu.VMEM((2 * SLOTS, width), F32)],
        compiler_params=params(),
        name="features",
    )(batch_index[None], points, frequencies, phases[None])

    pack = pl.pallas_call(
        functools.partial(project_kernel, n_out),
        grid=(steps,),
        out_shape=jax.ShapeDtypeStruct((n_chips, 32, 128), BF16),
        in_specs=[*weight_specs, feat_spec, whole((2 * SLOTS, width // 2))],
        out_specs=whole((n_chips, 32, 128)),
        scratch_shapes=[pltpu.VMEM((cols, own_features), F32)],
        compiler_params=params(),
        name="project",
    )(*weights, feats, sent_rows)
    got = lax.all_to_all(pack, CHIP_AXES, 0, 0)
    got_other = swap_core(got)

    key = batch_index * minibatch + lax.iota(jnp.int32, minibatch)
    rank = jnp.sum((key[None, :] < key[:, None]).astype(jnp.int32), 1)
    own_rank = lax.iota(jnp.int32, own_rows) * n_out + out
    chosen = own_rank[:, None] == rank[None, :]
    own_index = jnp.sum(jnp.where(chosen, batch_index[None, :], 0), 1)
    own_shard = own_index // rows
    starts = jnp.sum((own_index[None, :] < (own_shard * rows)[:, None]).astype(jnp.int32), 1)
    slot = lax.iota(jnp.int32, own_rows) - starts
    same_shard = (batch_index // rows)[None, :] == (batch_index // rows)[:, None]
    most = jnp.max(jnp.sum(same_shard.astype(jnp.int32), 1))
    overflow = most > SLOTS * n_out
    at = (own_shard // 2) * 32 + slot
    own_core = (own_shard % 2) == core
    at = jnp.stack([jnp.where(own_core, at, -64), jnp.where(own_core, -64, at)])
    at = jnp.broadcast_to(at[:, :, None], (2, own_rows, 128))
    col_norm = jnp.sum(jnp.square(points.astype(F32)), 1)[None]
    order = lax.rem(out - lax.iota(jnp.int32, n_out) + n_out, n_out)
    own_targets = jnp.einsum("im,qms->qsi", chosen.astype(F32), targets, precision=highest)[order]
    own_targets = own_targets.reshape(cols, own_rows)

    def gram(direct, where):
        return pl.pallas_call(
            functools.partial(gram_kernel, n_out, direct),
            grid=(steps,),
            out_shape=(
                jax.ShapeDtypeStruct((own_rows, rows), BF16),
                jax.ShapeDtypeStruct((cols // 2, own_rows), F32),
                jax.ShapeDtypeStruct((cols // 2, own_rows), F32),
                jax.ShapeDtypeStruct((8, 128), F32),
            ),
            in_specs=[
                *weight_specs,
                whole(where.shape),
                whole(got.shape),
                whole(got.shape),
                point_spec,
                pl.BlockSpec((1, BLOCK), lambda i: (0, i)),
            ],
            out_specs=(
                kern_spec,
                whole((cols // 2, own_rows)),
                whole((cols // 2, own_rows)),
                whole((8, 128)),
            ),
            scratch_shapes=[
                pltpu.VMEM((own_rows, width), BF16),
                pltpu.VMEM((own_rows, 128), F32),
                pltpu.VMEM((cols, own_rows), F32),
            ],
            compiler_params=params(),
            name="gram_fetched" if direct else "gram",
        )(*weights, where, got, got_other, points, col_norm)

    def fetch():
        local = own_index - shard * rows
        inside = (local >= 0) & (local < rows)
        picked = jnp.where(inside[:, None], points[jnp.clip(local, 0, rows - 1)].astype(F32), 0.0)
        return gram(True, lax.psum(picked, POINT_AXES).astype(BF16))

    kern, kept, given, tile = lax.cond(overflow, fetch, lambda: gram(False, at))

    pack = pl.pallas_call(
        pack_kernel,
        out_shape=jax.ShapeDtypeStruct((n_chips, cols // 2 + 16, 128), BF16),
        name="pack",
    )(kept, swap_core(given), tile)
    got = lax.all_to_all(pack, CHIP_AXES, 0, 0)
    got_other = swap_core(got)

    base, *parts = pl.pallas_call(
        functools.partial(step_kernel, n_out, ratio),
        grid=(steps,),
        out_shape=[jax.ShapeDtypeStruct((draws, rows), F32)]
        + [jax.ShapeDtypeStruct((draws, rows), BF16)] * (n_out - 1),
        in_specs=[
            pl.BlockSpec(memory_space=pltpu.SMEM),
            pl.BlockSpec(memory_space=pltpu.SMEM),
            whole(own_targets.shape),
            whole(got.shape),
            whole(got.shape),
            feat_spec,
            kern_spec,
            draw_spec,
        ],
        out_specs=[draw_spec] * n_out,
        scratch_shapes=[pltpu.VMEM((cols, own_features), BF16), pltpu.VMEM((cols, own_rows), BF16)],
        compiler_params=params(),
        name="step",
    )(coregion, noise_var, own_targets, got, got_other, feats, kern, own_weights)
    total = base
    for k, part in enumerate(parts, 1):
        part = lax.ppermute(part, "out", [(i, (i - k) % n_out) for i in range(n_out)])
        total = total + part.astype(F32)
    return total.T[None]


def solution(mesh):
    fine = Mesh(mesh.devices.reshape(8, 4, 2, 4), ("z", "y", "core", "out"))
    in_specs = (P(POINT_AXES, None), P("out", POINT_AXES, None), P(), P(), P(), P(), P(), P())
    out_specs = P("out", POINT_AXES, None)
    return jax.shard_map(shards, mesh=fine, in_specs=in_specs, out_specs=out_specs, check_vma=False)
```

```python
import functools
import math

import jax
import jax.numpy as jnp
from jax import lax
from jax.experimental import pallas as pl
from jax.experimental.pallas import tpu as pltpu
from jax.sharding import Mesh
from jax.sharding import PartitionSpec as P

LENGTH = 0.5
STEP_SIZE = 0.5
SLOTS = 8
CHUNK = 512
FEATURES_BLOCK = 1024
GRAM_BLOCK = 2048
STEP_BLOCK = 2048
SIN_TURNS = (
    6.283185160088695,
    -41.34165503124932,
    81.60100406363227,
    -76.54978208799582,
    39.53670460277009,
)
POINT_AXES = ("z", "y", "core")
CHIP_AXES = ("z", "y")
BF16 = jnp.bfloat16
F32 = jnp.float32
NT = (((1,), (1,)), ((), ()))


def dot(a, b):
    return jnp.dot(a, b, preferred_element_type=F32)


def dot_nt(a, b):
    return lax.dot_general(a, b, NT, preferred_element_type=F32)


def cos_turns(turns, scale):
    rest = turns - jnp.round(turns)
    quarter = 0.25 - jnp.abs(rest)
    square = quarter * quarter
    poly = F32(SIN_TURNS[-1] * scale)
    for coefficient in SIN_TURNS[-2::-1]:
        poly = poly * square + F32(coefficient * scale)
    return poly * quarter


def split(value):
    high = value.astype(BF16)
    return high, (value - high.astype(F32)).astype(BF16)


def place_of_device():
    chip = lax.axis_index("z") * lax.axis_size("y") + lax.axis_index("y")
    return lax.axis_index("out"), lax.axis_index("core"), chip


def whole(shape):
    return pl.BlockSpec(shape, lambda i: (0,) * len(shape))


def features_of(points, freq_ref, phase_ref, at, own):
    phase = phase_ref[:, pl.ds(at, own)] * (0.5 / math.pi)
    turns = dot(points, freq_ref[:, pl.ds(at, own)]) * (0.5 / math.pi) + phase
    return cos_turns(turns, math.sqrt(2.0 / freq_ref.shape[1])).astype(BF16)


def picked_rows(local, first, points):
    columns = lax.broadcasted_iota(jnp.int32, (2 * SLOTS, points.shape[0]), 1)
    return dot((local[:, :1] - first == columns).astype(F32).astype(BF16), points)


def features_kernel(shard_rows, index_ref, points_ref, freq_ref, phase_ref, feats_ref, local_ref, rows_ref):
    step = pl.program_id(0)
    out, core, chip = place_of_device()
    block = points_ref.shape[0]
    own = feats_ref.shape[1]
    n_out = freq_ref.shape[1] // own
    minibatch = index_ref.shape[1]

    @pl.when(step == 0)
    def _():
        base = (chip * 2 + core) * shard_rows
        index = index_ref[...]
        key = index * minibatch + lax.broadcasted_iota(jnp.int32, index.shape, 1)
        key_column = jnp.transpose(jnp.broadcast_to(key, (8, minibatch)))[:, :1]
        rank = jnp.sum((key_column < key).astype(jnp.int32), 0, keepdims=True)
        before = jnp.sum((index < base).astype(jnp.int32), 1, keepdims=True)
        first = (before - out + (n_out - 1)) // n_out
        inside = (index >= base) & (index < base + shard_rows) & (lax.rem(rank - out + n_out, n_out) == 0)
        slot = jnp.where(inside, (rank - out) // n_out - first, -1)
        here = slot == lax.broadcasted_iota(jnp.int32, (2 * SLOTS, minibatch), 0)
        local = jnp.sum(jnp.where(here, index - base + 1, 0), 1, keepdims=True) - 1
        local_ref[...] = jnp.broadcast_to(local, local_ref.shape)
        rows_ref[...] = jnp.zeros_like(rows_ref)

    points = points_ref[...]
    feats_ref[...] = features_of(points, freq_ref, phase_ref, pl.multiple_of(out * own, own), own)
    rows_ref[...] += picked_rows(local_ref[...], step * block, points)


def project_kernel(n_out, *refs):
    weight_refs = refs[:n_out]
    points_ref, freq_ref, phase_ref, local_ref, early_ref, earlier_ref = refs[n_out : n_out + 6]
    feats_ref, pack_ref, sum_ref, rows_ref = refs[n_out + 6 :]
    step = pl.program_id(0)
    steps = pl.num_programs(0)
    block = points_ref.shape[0]
    own = feats_ref.shape[1]

    @pl.when(step == 0)
    def _():
        sum_ref[...] = jnp.zeros_like(sum_ref)
        rows_ref[...] = earlier_ref[...]

    def weights(at):
        here = pl.ds(pl.multiple_of(at * block, block), block)
        return jnp.concatenate([ref[:, here] for ref in weight_refs], 0)

    points = points_ref[...]
    at = pl.multiple_of(lax.axis_index("out") * own, own)
    feats = features_of(points, freq_ref, phase_ref, at, own)
    feats_ref[...] = feats
    rows_ref[...] += picked_rows(local_ref[...], (step + steps) * block, points)
    sum_ref[...] += dot(weights(step), early_ref[...]) + dot(weights(step + steps), feats)

    @pl.when(step == steps - 1)
    def _():
        half = rows_ref.shape[1] // 2
        rows = rows_ref[...]
        rows = jnp.concatenate([rows[:SLOTS, :half], rows[:SLOTS, half:]], 0).astype(BF16)
        across = own // 128
        for at in range(pack_ref.shape[0]):
            r, c = divmod(at, across)
            high, low = split(sum_ref[8 * r : 8 * r + 8, 128 * c : 128 * c + 128])
            pack_ref[at, :16] = rows
            pack_ref[at, 16:] = jnp.concatenate([high.astype(F32), low.astype(F32)], 0).astype(BF16)


def gram_kernel(n_out, direct, *refs):
    weight_refs = refs[:n_out]
    at_ref, own_ref, other_ref, points_ref, norm_ref = refs[n_out : n_out + 5]
    kern_ref, kept_ref, given_ref, tile_ref, rows_ref, row_norm_ref, sum_ref = refs[n_out + 5 :]
    step = pl.program_id(0)

    @pl.when(step == 0)
    def _():
        peers, height, lanes = own_ref.shape
        if direct:
            rows = at_ref[...].astype(F32)
        else:
            columns = lax.broadcasted_iota(jnp.int32, (rows_ref.shape[0], peers * height), 1)
            halves = []
            for half in range(2):
                part = 0.0
                for source, held in enumerate((own_ref, other_ref)):
                    pick = (at_ref[source][:, :1] + half * SLOTS == columns).astype(F32).astype(BF16)
                    part = part + dot(pick, held[...].reshape(peers * height, lanes))
                halves.append(part)
            rows = jnp.concatenate(halves, 1)
        rows_ref[...] = rows.astype(BF16)
        row_norm_ref[...] = jnp.broadcast_to(jnp.sum(rows * rows, 1, keepdims=True), row_norm_ref.shape)
        sum_ref[...] = jnp.zeros_like(sum_ref)
        tile = jnp.sum(own_ref[:, 16:].astype(F32), 0) + jnp.sum(other_ref[:, 16:].astype(F32), 0)
        high, low = split(tile[:8] + tile[8:])
        tile_ref[...] = jnp.concatenate([high.astype(F32), low.astype(F32)], 0).astype(BF16)

    total = 0.0
    for at in range(0, points_ref.shape[0], CHUNK):
        here = pl.ds(at, CHUNK)
        inner = dot_nt(rows_ref[...], points_ref[here, :])
        squared = row_norm_ref[:, :1] + norm_ref[:, here] - 2.0 * inner
        scaled_square = (5.0 / (LENGTH * LENGTH)) * jnp.maximum(squared, 0.0)
        scaled_r = scaled_square * lax.rsqrt(jnp.maximum(scaled_square, 1e-30))
        kern = (1.0 + scaled_r + scaled_square * (1.0 / 3.0)) * jnp.exp(-scaled_r)
        kern = kern.astype(BF16)
        kern_ref[:, here] = kern
        weights = jnp.concatenate([ref[:, here] for ref in weight_refs], 0)
        total = total + dot_nt(weights, kern)
    sum_ref[...] += total

    @pl.when(step == pl.num_programs(0) - 1)
    def _():
        half = kept_ref.shape[0]
        core = lax.axis_index("core")
        lower, upper = sum_ref[:half], sum_ref[half:]
        kept_ref[...] = jnp.where(core == 0, lower, upper)
        given_ref[...] = jnp.where(core == 0, upper, lower)


def step_kernel(n_out, ratio, *refs):
    coregion_ref, noise_ref, targets_ref, own_ref, other_ref, feats_ref, kern_ref = refs[:7]
    base_ref, part_refs, (mixed_ref, weighted_ref) = refs[7], refs[8 : 7 + n_out], refs[7 + n_out :]
    draws = base_ref.shape[0]
    half = n_out * draws // 2

    @pl.when(pl.program_id(0) == 0)
    def _():
        out, core, _ = place_of_device()
        order = [lax.rem(out - k + n_out, n_out) for k in range(n_out)]
        mixer = [[coregion_ref[a, b] for b in order] for a in order]

        def mix(values):
            return [sum(c * v for c, v in zip(line, values)) for line in mixer]

        own = jnp.sum(own_ref[:, :half].astype(F32), 0)
        other = jnp.sum(other_ref[:, :half].astype(F32), 0)
        total = jnp.concatenate([jnp.where(core == 0, own, other), jnp.where(core == 0, other, own)], 0)
        fitted = mix([total[draws * k : draws * (k + 1)] for k in range(n_out)])
        scaled = [
            (fitted[k] - targets_ref[draws * k : draws * (k + 1)]) / noise_ref[order[k]] for k in range(n_out)
        ]
        weighted = jnp.concatenate(mix(scaled), 0).astype(BF16)
        weighted_ref[...] = (weighted.astype(F32) * ratio).astype(BF16)
        across = mixed_ref.shape[1] // 128
        tiles = [own_ref[p, half:].astype(F32) for p in range(own_ref.shape[0])]
        tiles = [tile[:8] + tile[8:] for tile in tiles]
        lines = [
            jnp.concatenate(tiles[across * r : across * (r + 1)], 1) for r in range(n_out * draws // 8)
        ]
        each = draws // 8
        projected = [jnp.concatenate(lines[each * k : each * (k + 1)], 0) for k in range(n_out)]
        mixed_ref[...] = jnp.concatenate(mix(projected), 0).astype(BF16)

    gradient = dot(weighted_ref[...], kern_ref[...]) + dot_nt(mixed_ref[...], feats_ref[...])
    change = -STEP_SIZE * gradient
    base_ref[...] = change[:draws]
    for k, ref in enumerate(part_refs, 1):
        ref[...] = change[draws * k : draws * (k + 1)].astype(BF16)


def swap_core(value):
    return lax.ppermute(value, "core", [(0, 1), (1, 0)])


def params(limit=None):
    return pltpu.CompilerParams(dimension_semantics=("arbitrary",), vmem_limit_bytes=limit)


def shards(points, rep_weights, batch_index, targets, noise_var, coregion, frequencies, phases):
    highest = lax.Precision.HIGHEST
    n_out = lax.axis_size("out")
    n_chips = lax.axis_size("z") * lax.axis_size("y")
    n_pts = 2 * n_chips
    rows, width = points.shape
    draws = rep_weights.shape[2]
    minibatch = batch_index.shape[0]
    own_rows = minibatch // n_out
    own_features = frequencies.shape[1] // n_out
    cols = n_out * draws
    out, core, chip = place_of_device()
    shard = chip * 2 + core
    ratio = (rows * n_pts) / minibatch

    own_weights = rep_weights[0].T
    low = own_weights.astype(BF16)
    weights = [low]
    for k in range(1, n_out):
        weights.append(lax.ppermute(low, "out", [(i, (i + k) % n_out) for i in range(n_out)]))
    weight_specs = lambda block: [pl.BlockSpec((draws, block), lambda i: (0, i))] * n_out
    point_spec = lambda block: pl.BlockSpec((block, width), lambda i: (i, 0))
    feat_spec = lambda block: pl.BlockSpec((block, own_features), lambda i: (i, 0))
    kern_spec = lambda block: pl.BlockSpec((own_rows, block), lambda i: (0, i))
    draw_spec = lambda block: pl.BlockSpec((draws, block), lambda i: (0, i))

    early = rows // 2 // FEATURES_BLOCK
    feats, local, picked = pl.pallas_call(
        functools.partial(features_kernel, rows),
        grid=(early,),
        out_shape=(
            jax.ShapeDtypeStruct((rows, own_features), BF16),
            jax.ShapeDtypeStruct((2 * SLOTS, 128), jnp.int32),
            jax.ShapeDtypeStruct((2 * SLOTS, width), F32),
        ),
        in_specs=[
            whole((1, minibatch)),
            point_spec(FEATURES_BLOCK),
            whole(frequencies.shape),
            whole((1, phases.shape[0])),
        ],
        out_specs=(feat_spec(FEATURES_BLOCK), whole((2 * SLOTS, 128)), whole((2 * SLOTS, width))),
        compiler_params=params(),
        name="features",
    )(batch_index[None], points, frequencies, phases[None])

    feats, pack = pl.pallas_call(
        functools.partial(project_kernel, n_out),
        grid=(early,),
        out_shape=(
            jax.ShapeDtypeStruct((rows, own_features), BF16),
            jax.ShapeDtypeStruct((n_chips, 32, 128), BF16),
        ),
        in_specs=[whole((draws, rows))] * n_out
        + [
            pl.BlockSpec((FEATURES_BLOCK, width), lambda i: (i + early, 0)),
            whole(frequencies.shape),
            whole((1, phases.shape[0])),
            whole((2 * SLOTS, 128)),
            feat_spec(FEATURES_BLOCK),
            whole((2 * SLOTS, width)),
        ],
        out_specs=(
            pl.BlockSpec((FEATURES_BLOCK, own_features), lambda i: (i + early, 0)),
            whole((n_chips, 32, 128)),
        ),
        scratch_shapes=[pltpu.VMEM((cols, own_features), F32), pltpu.VMEM((2 * SLOTS, width), F32)],
        input_output_aliases={n_out + 4: 0},
        compiler_params=params(),
        name="project",
    )(*weights, points, frequencies, phases[None], local, feats, picked)
    got = lax.all_to_all(pack, CHIP_AXES, 0, 0)
    batch_index, points_now, targets, _ = lax.optimization_barrier((batch_index, points, targets, pack))

    key = batch_index * minibatch + lax.iota(jnp.int32, minibatch)
    rank = jnp.sum((key[None, :] < key[:, None]).astype(jnp.int32), 1)
    own_rank = lax.iota(jnp.int32, own_rows) * n_out + out
    chosen = own_rank[:, None] == rank[None, :]
    own_index = jnp.sum(jnp.where(chosen, batch_index[None, :], 0), 1)
    own_shard = own_index // rows
    starts = jnp.sum((own_index[None, :] < (own_shard * rows)[:, None]).astype(jnp.int32), 1)
    slot = lax.iota(jnp.int32, own_rows) - starts
    same_shard = (batch_index // rows)[None, :] == (batch_index // rows)[:, None]
    most = jnp.max(jnp.sum(same_shard.astype(jnp.int32), 1))
    overflow = most > SLOTS * n_out
    at = (own_shard // 2) * 32 + slot
    own_core = (own_shard % 2) == core
    at = jnp.stack([jnp.where(own_core, at, -64), jnp.where(own_core, -64, at)])
    at = jnp.broadcast_to(at[:, :, None], (2, own_rows, 128))
    col_norm = jnp.sum(jnp.square(points_now.astype(F32)), 1)[None]
    order = lax.rem(out - lax.iota(jnp.int32, n_out) + n_out, n_out)
    own_targets = jnp.einsum("im,qms->qsi", chosen.astype(F32), targets, precision=highest)[order]
    own_targets = own_targets.reshape(cols, own_rows)
    got, at, overflow, own_index, col_norm, own_targets = lax.optimization_barrier(
        (got, at, overflow, own_index, col_norm, own_targets)
    )
    got_other = swap_core(got)

    def gram(direct, where):
        return pl.pallas_call(
            functools.partial(gram_kernel, n_out, direct),
            grid=(rows // GRAM_BLOCK,),
            out_shape=(
                jax.ShapeDtypeStruct((own_rows, rows), BF16),
                jax.ShapeDtypeStruct((cols // 2, own_rows), F32),
                jax.ShapeDtypeStruct((cols // 2, own_rows), F32),
                jax.ShapeDtypeStruct((16, 128), BF16),
            ),
            in_specs=[
                *weight_specs(GRAM_BLOCK),
                whole(where.shape),
                whole(got.shape),
                whole(got.shape),
                point_spec(GRAM_BLOCK),
                pl.BlockSpec((1, GRAM_BLOCK), lambda i: (0, i)),
            ],
            out_specs=(
                kern_spec(GRAM_BLOCK),
                whole((cols // 2, own_rows)),
                whole((cols // 2, own_rows)),
                whole((16, 128)),
            ),
            scratch_shapes=[
                pltpu.VMEM((own_rows, width), BF16),
                pltpu.VMEM((own_rows, 128), F32),
                pltpu.VMEM((cols, own_rows), F32),
            ],
            compiler_params=params(24 * 1024 * 1024),
            name="gram_fetched" if direct else "gram",
        )(*weights, where, got, got_other, points, col_norm)

    def fetch():
        local = own_index - shard * rows
        inside = (local >= 0) & (local < rows)
        picked = jnp.where(inside[:, None], points[jnp.clip(local, 0, rows - 1)].astype(F32), 0.0)
        return gram(True, lax.psum(picked, POINT_AXES).astype(BF16))

    kern, kept, given, tile = lax.cond(overflow, fetch, lambda: gram(False, at))

    pack = jnp.concatenate([(kept + swap_core(given)).astype(BF16), tile], 0)
    pack = jnp.broadcast_to(pack[None], (n_chips, *pack.shape))
    got = lax.all_to_all(pack, CHIP_AXES, 0, 0)
    got_other = swap_core(got)

    base, *parts = pl.pallas_call(
        functools.partial(step_kernel, n_out, ratio),
        grid=(rows // STEP_BLOCK,),
        out_shape=[jax.ShapeDtypeStruct((draws, rows), F32)]
        + [jax.ShapeDtypeStruct((draws, rows), BF16)] * (n_out - 1),
        in_specs=[
            pl.BlockSpec(memory_space=pltpu.SMEM),
            pl.BlockSpec(memory_space=pltpu.SMEM),
            whole(own_targets.shape),
            whole(got.shape),
            whole(got.shape),
            feat_spec(STEP_BLOCK),
            kern_spec(STEP_BLOCK),
        ],
        out_specs=[draw_spec(STEP_BLOCK)] * n_out,
        scratch_shapes=[pltpu.VMEM((cols, own_features), BF16), pltpu.VMEM((cols, own_rows), BF16)],
        compiler_params=params(24 * 1024 * 1024),
        name="step",
    )(coregion, noise_var, own_targets, got, got_other, feats, kern)
    total = own_weights + base
    for k, part in enumerate(parts, 1):
        part = lax.ppermute(part, "out", [(i, (i - k) % n_out) for i in range(n_out)])
        total = total + part.astype(F32)
    return total.T[None]


def solution(mesh):
    fine = Mesh(mesh.devices.reshape(8, 4, 2, 4), ("z", "y", "core", "out"))
    in_specs = (P(POINT_AXES, None), P("out", POINT_AXES, None), P(), P(), P(), P(), P(), P())
    out_specs = P("out", POINT_AXES, None)
    return jax.shard_map(shards, mesh=fine, in_specs=in_specs, out_specs=out_specs, check_vma=False)
```

```python
import functools
import math

import jax
import jax.numpy as jnp
from jax import lax
from jax.experimental import pallas as pl
from jax.experimental.pallas import tpu as pltpu
from jax.sharding import Mesh
from jax.sharding import PartitionSpec as P

LENGTH = 0.5
STEP_SIZE = 0.5
SLOTS = 8
CHUNK = 512
FEATURES_BLOCK = 1024
GRAM_BLOCK = 2048
STEP_BLOCK = 2048
SMALL_VMEM = 24 * 1024 * 1024
SIN_TURNS = (
    6.283185160088695,
    -41.34165503124932,
    81.60100406363227,
    -76.54978208799582,
    39.53670460277009,
)
POINT_AXES = ("z", "y", "core")
CHIP_AXES = ("z", "y")
BF16 = jnp.bfloat16
F32 = jnp.float32
NT = (((1,), (1,)), ((), ()))


def dot(a, b):
    return jnp.dot(a, b, preferred_element_type=F32)


def dot_nt(a, b):
    return lax.dot_general(a, b, NT, preferred_element_type=F32)


def cos_turns(turns, scale):
    rest = turns - jnp.round(turns)
    quarter = 0.25 - jnp.abs(rest)
    square = quarter * quarter
    poly = F32(SIN_TURNS[-1] * scale)
    for coefficient in SIN_TURNS[-2::-1]:
        poly = poly * square + F32(coefficient * scale)
    return poly * quarter


def split(value):
    high = value.astype(BF16)
    return high, (value - high.astype(F32)).astype(BF16)


def place_of_device():
    chip = lax.axis_index("z") * lax.axis_size("y") + lax.axis_index("y")
    return lax.axis_index("out"), lax.axis_index("core"), chip


def whole(shape):
    return pl.BlockSpec(shape, lambda i: (0,) * len(shape))


def features_of(points, freq_ref, phase_ref, at, own):
    phase = phase_ref[:, pl.ds(at, own)] * (0.5 / math.pi)
    turns = dot(points, freq_ref[:, pl.ds(at, own)]) * (0.5 / math.pi) + phase
    return cos_turns(turns, math.sqrt(2.0 / freq_ref.shape[1])).astype(BF16)


def picked_rows(local, first, points):
    columns = lax.broadcasted_iota(jnp.int32, (2 * SLOTS, points.shape[0]), 1)
    return dot((local[:, :1] - first == columns).astype(F32).astype(BF16), points)


def features_kernel(index_ref, points_ref, freq_ref, phase_ref, feats_ref, held_ref, sent_ref, local_ref, rows_ref):
    step = pl.program_id(0)
    out, core, chip = place_of_device()
    block = points_ref.shape[0]
    own = feats_ref.shape[1]
    n_out = freq_ref.shape[1] // own
    shard_rows = held_ref.shape[0]
    minibatch = index_ref.shape[1]

    @pl.when(step == 0)
    def _():
        base = (chip * 2 + core) * shard_rows
        index = index_ref[...]
        key = index * minibatch + lax.broadcasted_iota(jnp.int32, index.shape, 1)
        key_column = jnp.transpose(jnp.broadcast_to(key, (8, minibatch)))[:, :1]
        rank = jnp.sum((key_column < key).astype(jnp.int32), 0, keepdims=True)
        before = jnp.sum((index < base).astype(jnp.int32), 1, keepdims=True)
        first = (before - out + (n_out - 1)) // n_out
        inside = (index >= base) & (index < base + shard_rows) & (lax.rem(rank - out + n_out, n_out) == 0)
        slot = jnp.where(inside, (rank - out) // n_out - first, -1)
        here = slot == lax.broadcasted_iota(jnp.int32, (2 * SLOTS, minibatch), 0)
        local = jnp.sum(jnp.where(here, index - base + 1, 0), 1, keepdims=True) - 1
        local_ref[...] = jnp.broadcast_to(local, local_ref.shape)
        rows_ref[...] = jnp.zeros_like(rows_ref)

    points = points_ref[...]
    at = pl.multiple_of(out * own, own)
    phase = phase_ref[:, pl.ds(at, own)] * (0.5 / math.pi)
    turns = dot(points, freq_ref[:, pl.ds(at, own)]) * (0.5 / math.pi) + phase
    feats = cos_turns(turns, math.sqrt(2.0 / freq_ref.shape[1])).astype(BF16)
    feats_ref[...] = feats
    held_ref[pl.ds(pl.multiple_of(step * block, block), block), :] = feats
    columns = lax.broadcasted_iota(jnp.int32, (2 * SLOTS, block), 1)
    rows_ref[...] += dot((local_ref[:, :1] - step * block == columns).astype(F32).astype(BF16), points)

    @pl.when(step == pl.num_programs(0) - 1)
    def _():
        half = rows_ref.shape[1] // 2
        rows = rows_ref[...]
        sent_ref[...] = jnp.concatenate([rows[:SLOTS, :half], rows[:SLOTS, half:]], 0).astype(BF16)


def project_kernel(n_out, *refs):
    weight_refs, (feats_ref, sent_ref, pack_ref) = refs[:n_out], refs[n_out:]
    total = dot(jnp.concatenate([ref[...] for ref in weight_refs], 0), feats_ref[...])
    across = total.shape[1] // 128
    for at in range(pack_ref.shape[0]):
        r, c = divmod(at, across)
        high, low = split(total[8 * r : 8 * r + 8, 128 * c : 128 * c + 128])
        pack_ref[at, :16] = sent_ref[...]
        pack_ref[at, 16:] = jnp.concatenate([high.astype(F32), low.astype(F32)], 0).astype(BF16)


def gram_kernel(n_out, direct, *refs):
    weight_refs = refs[:n_out]
    at_ref, own_ref, other_ref, points_ref, norm_ref = refs[n_out : n_out + 5]
    kern_ref, kept_ref, given_ref, tile_ref, rows_ref, row_norm_ref, sum_ref = refs[n_out + 5 :]
    step = pl.program_id(0)

    @pl.when(step == 0)
    def _():
        peers, height, lanes = own_ref.shape
        if direct:
            rows = at_ref[...].astype(F32)
        else:
            columns = lax.broadcasted_iota(jnp.int32, (rows_ref.shape[0], peers * height), 1)
            halves = []
            for half in range(2):
                part = 0.0
                for source, held in enumerate((own_ref, other_ref)):
                    pick = (at_ref[source][:, :1] + half * SLOTS == columns).astype(F32).astype(BF16)
                    part = part + dot(pick, held[...].reshape(peers * height, lanes))
                halves.append(part)
            rows = jnp.concatenate(halves, 1)
        rows_ref[...] = rows.astype(BF16)
        row_norm_ref[...] = jnp.broadcast_to(jnp.sum(rows * rows, 1, keepdims=True), row_norm_ref.shape)
        sum_ref[...] = jnp.zeros_like(sum_ref)
        tile = jnp.sum(own_ref[:, 16:].astype(F32), 0) + jnp.sum(other_ref[:, 16:].astype(F32), 0)
        high, low = split(tile[:8] + tile[8:])
        tile_ref[...] = jnp.concatenate([high.astype(F32), low.astype(F32)], 0).astype(BF16)

    total = 0.0
    for at in range(0, points_ref.shape[0], CHUNK):
        here = pl.ds(at, CHUNK)
        inner = dot_nt(rows_ref[...], points_ref[here, :])
        squared = row_norm_ref[:, :1] + norm_ref[:, here] - 2.0 * inner
        scaled_square = (5.0 / (LENGTH * LENGTH)) * jnp.maximum(squared, 0.0)
        scaled_r = scaled_square * lax.rsqrt(jnp.maximum(scaled_square, 1e-30))
        kern = (1.0 + scaled_r + scaled_square * (1.0 / 3.0)) * jnp.exp(-scaled_r)
        kern = kern.astype(BF16)
        kern_ref[:, here] = kern
        weights = jnp.concatenate([ref[:, here] for ref in weight_refs], 0)
        total = total + dot_nt(weights, kern)
    sum_ref[...] += total

    @pl.when(step == pl.num_programs(0) - 1)
    def _():
        half = kept_ref.shape[0]
        core = lax.axis_index("core")
        lower, upper = sum_ref[:half], sum_ref[half:]
        kept_ref[...] = jnp.where(core == 0, lower, upper)
        given_ref[...] = jnp.where(core == 0, upper, lower)


def step_kernel(n_out, ratio, *refs):
    coregion_ref, noise_ref, targets_ref, own_ref, other_ref, feats_ref, kern_ref = refs[:7]
    base_ref, part_refs, (mixed_ref, weighted_ref) = refs[7], refs[8 : 7 + n_out], refs[7 + n_out :]
    draws = base_ref.shape[0]
    half = n_out * draws // 2

    @pl.when(pl.program_id(0) == 0)
    def _():
        out, core, _ = place_of_device()
        order = [lax.rem(out - k + n_out, n_out) for k in range(n_out)]
        mixer = [[coregion_ref[a, b] for b in order] for a in order]

        def mix(values):
            return [sum(c * v for c, v in zip(line, values)) for line in mixer]

        own = jnp.sum(own_ref[:, :half].astype(F32), 0)
        other = jnp.sum(other_ref[:, :half].astype(F32), 0)
        total = jnp.concatenate([jnp.where(core == 0, own, other), jnp.where(core == 0, other, own)], 0)
        fitted = mix([total[draws * k : draws * (k + 1)] for k in range(n_out)])
        scaled = [
            (fitted[k] - targets_ref[draws * k : draws * (k + 1)]) / noise_ref[order[k]] for k in range(n_out)
        ]
        weighted = jnp.concatenate(mix(scaled), 0).astype(BF16)
        weighted_ref[...] = (weighted.astype(F32) * ratio).astype(BF16)
        across = mixed_ref.shape[1] // 128
        tiles = [own_ref[p, half:].astype(F32) for p in range(own_ref.shape[0])]
        tiles = [tile[:8] + tile[8:] for tile in tiles]
        lines = [
            jnp.concatenate(tiles[across * r : across * (r + 1)], 1) for r in range(n_out * draws // 8)
        ]
        each = draws // 8
        projected = [jnp.concatenate(lines[each * k : each * (k + 1)], 0) for k in range(n_out)]
        mixed_ref[...] = jnp.concatenate(mix(projected), 0).astype(BF16)

    gradient = dot(weighted_ref[...], kern_ref[...]) + dot_nt(mixed_ref[...], feats_ref[...])
    change = -STEP_SIZE * gradient
    base_ref[...] = change[:draws]
    for k, ref in enumerate(part_refs, 1):
        ref[...] = change[draws * k : draws * (k + 1)].astype(BF16)


def in_hbm(value):
    return pltpu.with_memory_space_constraint(value, pltpu.HBM)


def swap_core(value):
    return lax.ppermute(value, "core", [(0, 1), (1, 0)])


def params(limit=None):
    return pltpu.CompilerParams(dimension_semantics=("arbitrary",), vmem_limit_bytes=limit)


def shards(points, rep_weights, batch_index, targets, noise_var, coregion, frequencies, phases):
    highest = lax.Precision.HIGHEST
    n_out = lax.axis_size("out")
    n_chips = lax.axis_size("z") * lax.axis_size("y")
    n_pts = 2 * n_chips
    rows, width = points.shape
    draws = rep_weights.shape[2]
    minibatch = batch_index.shape[0]
    own_rows = minibatch // n_out
    own_features = frequencies.shape[1] // n_out
    cols = n_out * draws
    out, core, chip = place_of_device()
    shard = chip * 2 + core
    ratio = (rows * n_pts) / minibatch

    own_weights = rep_weights[0].T
    low = own_weights.astype(BF16)
    weights = [low]
    for k in range(1, n_out):
        weights.append(lax.ppermute(low, "out", [(i, (i + k) % n_out) for i in range(n_out)]))
    weight_specs = lambda block: [pl.BlockSpec((draws, block), lambda i: (0, i))] * n_out
    point_spec = lambda block: pl.BlockSpec((block, width), lambda i: (i, 0))
    feat_spec = lambda block: pl.BlockSpec((block, own_features), lambda i: (i, 0))
    kern_spec = lambda block: pl.BlockSpec((own_rows, block), lambda i: (0, i))
    draw_spec = lambda block: pl.BlockSpec((draws, block), lambda i: (0, i))

    feats, held, sent_rows = pl.pallas_call(
        features_kernel,
        grid=(rows // FEATURES_BLOCK,),
        out_shape=(
            pltpu.HBM((rows, own_features), BF16),
            pltpu.VMEM((rows, own_features), BF16),
            jax.ShapeDtypeStruct((2 * SLOTS, width // 2), BF16),
        ),
        in_specs=[
            whole((1, minibatch)),
            point_spec(FEATURES_BLOCK),
            whole(frequencies.shape),
            whole((1, phases.shape[0])),
        ],
        out_specs=(
            feat_spec(FEATURES_BLOCK),
            pl.BlockSpec(memory_space=pltpu.VMEM),
            whole((2 * SLOTS, width // 2)),
        ),
        scratch_shapes=[pltpu.VMEM((2 * SLOTS, 128), jnp.int32), pltpu.VMEM((2 * SLOTS, width), F32)],
        compiler_params=params(SMALL_VMEM),
        name="features",
    )(in_hbm(batch_index[None]), in_hbm(points), in_hbm(frequencies), in_hbm(phases[None]))

    in_vmem = pl.BlockSpec(memory_space=pltpu.VMEM)
    pack = pl.pallas_call(
        functools.partial(project_kernel, n_out),
        out_shape=jax.ShapeDtypeStruct((n_chips, 32, 128), BF16),
        in_specs=[in_vmem] * (n_out + 2),
        out_specs=in_vmem,
        compiler_params=pltpu.CompilerParams(vmem_limit_bytes=SMALL_VMEM),
        name="project",
    )(*weights, pltpu.with_memory_space_constraint(held, pltpu.VMEM), sent_rows)
    got = lax.all_to_all(pack, CHIP_AXES, 0, 0)
    batch_index, points_now, targets, _ = lax.optimization_barrier((batch_index, points, targets, pack))

    key = batch_index * minibatch + lax.iota(jnp.int32, minibatch)
    rank = jnp.sum((key[None, :] < key[:, None]).astype(jnp.int32), 1)
    own_rank = lax.iota(jnp.int32, own_rows) * n_out + out
    chosen = own_rank[:, None] == rank[None, :]
    own_index = jnp.sum(jnp.where(chosen, batch_index[None, :], 0), 1)
    own_shard = own_index // rows
    starts = jnp.sum((own_index[None, :] < (own_shard * rows)[:, None]).astype(jnp.int32), 1)
    slot = lax.iota(jnp.int32, own_rows) - starts
    same_shard = (batch_index // rows)[None, :] == (batch_index // rows)[:, None]
    most = jnp.max(jnp.sum(same_shard.astype(jnp.int32), 1))
    overflow = most > SLOTS * n_out
    at = (own_shard // 2) * 32 + slot
    own_core = (own_shard % 2) == core
    at = jnp.stack([jnp.where(own_core, at, -64), jnp.where(own_core, -64, at)])
    at = jnp.broadcast_to(at[:, :, None], (2, own_rows, 128))
    col_norm = jnp.sum(jnp.square(points_now.astype(F32)), 1)[None]
    order = lax.rem(out - lax.iota(jnp.int32, n_out) + n_out, n_out)
    own_targets = jnp.einsum("im,qms->qsi", chosen.astype(F32), targets, precision=highest)[order]
    own_targets = own_targets.reshape(cols, own_rows)
    got, at, overflow, own_index, col_norm, own_targets = lax.optimization_barrier(
        (got, at, overflow, own_index, col_norm, own_targets)
    )
    got_other = swap_core(got)

    def gram(direct, where):
        return pl.pallas_call(
            functools.partial(gram_kernel, n_out, direct),
            grid=(rows // GRAM_BLOCK,),
            out_shape=(
                jax.ShapeDtypeStruct((own_rows, rows), BF16),
                jax.ShapeDtypeStruct((cols // 2, own_rows), F32),
                jax.ShapeDtypeStruct((cols // 2, own_rows), F32),
                jax.ShapeDtypeStruct((16, 128), BF16),
            ),
            in_specs=[
                *weight_specs(GRAM_BLOCK),
                whole(where.shape),
                whole(got.shape),
                whole(got.shape),
                point_spec(GRAM_BLOCK),
                pl.BlockSpec((1, GRAM_BLOCK), lambda i: (0, i)),
            ],
            out_specs=(
                kern_spec(GRAM_BLOCK),
                whole((cols // 2, own_rows)),
                whole((cols // 2, own_rows)),
                whole((16, 128)),
            ),
            scratch_shapes=[
                pltpu.VMEM((own_rows, width), BF16),
                pltpu.VMEM((own_rows, 128), F32),
                pltpu.VMEM((cols, own_rows), F32),
            ],
            compiler_params=params(SMALL_VMEM),
            name="gram_fetched" if direct else "gram",
        )(*weights, where, got, got_other, points, col_norm)

    def fetch():
        local = own_index - shard * rows
        inside = (local >= 0) & (local < rows)
        picked = jnp.where(inside[:, None], points[jnp.clip(local, 0, rows - 1)].astype(F32), 0.0)
        return gram(True, lax.psum(picked, POINT_AXES).astype(BF16))

    kern, kept, given, tile = lax.cond(overflow, fetch, lambda: gram(False, at))

    pack = jnp.concatenate([(kept + swap_core(given)).astype(BF16), tile], 0)
    pack = jnp.broadcast_to(pack[None], (n_chips, *pack.shape))
    got = lax.all_to_all(pack, CHIP_AXES, 0, 0)
    got_other = swap_core(got)

    base, *parts = pl.pallas_call(
        functools.partial(step_kernel, n_out, ratio),
        grid=(rows // STEP_BLOCK,),
        out_shape=[jax.ShapeDtypeStruct((draws, rows), F32)]
        + [jax.ShapeDtypeStruct((draws, rows), BF16)] * (n_out - 1),
        in_specs=[
            pl.BlockSpec(memory_space=pltpu.SMEM),
            pl.BlockSpec(memory_space=pltpu.SMEM),
            whole(own_targets.shape),
            whole(got.shape),
            whole(got.shape),
            feat_spec(STEP_BLOCK),
            kern_spec(STEP_BLOCK),
        ],
        out_specs=[draw_spec(STEP_BLOCK)] * n_out,
        scratch_shapes=[pltpu.VMEM((cols, own_features), BF16), pltpu.VMEM((cols, own_rows), BF16)],
        compiler_params=params(SMALL_VMEM),
        name="step",
    )(coregion, noise_var, own_targets, got, got_other, in_hbm(feats), in_hbm(kern))
    total = own_weights + base
    for k, part in enumerate(parts, 1):
        part = lax.ppermute(part, "out", [(i, (i - k) % n_out) for i in range(n_out)])
        total = total + part.astype(F32)
    return total.T[None]


def solution(mesh):
    fine = Mesh(mesh.devices.reshape(8, 4, 2, 4), ("z", "y", "core", "out"))
    in_specs = (P(POINT_AXES, None), P("out", POINT_AXES, None), P(), P(), P(), P(), P(), P())
    out_specs = P("out", POINT_AXES, None)
    return jax.shard_map(shards, mesh=fine, in_specs=in_specs, out_specs=out_specs, check_vma=False)
```

```python
import functools
import math

import jax
import jax.numpy as jnp
from jax import lax
from jax.experimental import pallas as pl
from jax.experimental.pallas import tpu as pltpu
from jax.sharding import Mesh
from jax.sharding import PartitionSpec as P

LENGTH = 0.5
STEP_SIZE = 0.5
SLOTS = 8
CHUNK = 1024
FEATURES_BLOCK = 1024
STEP_BLOCK = 2048
SMALL_VMEM = 24 * 1024 * 1024
SIN_TURNS = (
    6.283185160088695,
    -41.34165503124932,
    81.60100406363227,
    -76.54978208799582,
    39.53670460277009,
)
POINT_AXES = ("z", "y", "core")
CHIP_AXES = ("z", "y")
BF16 = jnp.bfloat16
F32 = jnp.float32
NT = (((1,), (1,)), ((), ()))


def dot(a, b):
    return jnp.dot(a, b, preferred_element_type=F32)


def dot_nt(a, b):
    return lax.dot_general(a, b, NT, preferred_element_type=F32)


def cos_turns(turns, scale):
    rest = turns - jnp.round(turns)
    quarter = 0.25 - jnp.abs(rest)
    square = quarter * quarter
    poly = F32(SIN_TURNS[-1] * scale)
    for coefficient in SIN_TURNS[-2::-1]:
        poly = poly * square + F32(coefficient * scale)
    return poly * quarter


def split(value):
    high = value.astype(BF16)
    return high, (value - high.astype(F32)).astype(BF16)


def place_of_device():
    chip = lax.axis_index("z") * lax.axis_size("y") + lax.axis_index("y")
    return lax.axis_index("out"), lax.axis_index("core"), chip


def whole(shape):
    return pl.BlockSpec(shape, lambda i: (0,) * len(shape))


def features_of(points, freq_ref, phase_ref, at, own):
    phase = phase_ref[:, pl.ds(at, own)] * (0.5 / math.pi)
    turns = dot(points, freq_ref[:, pl.ds(at, own)]) * (0.5 / math.pi) + phase
    return cos_turns(turns, math.sqrt(2.0 / freq_ref.shape[1])).astype(BF16)


def picked_rows(local, first, points):
    columns = lax.broadcasted_iota(jnp.int32, (2 * SLOTS, points.shape[0]), 1)
    return dot((local[:, :1] - first == columns).astype(F32).astype(BF16), points)


def features_kernel(index_ref, points_ref, freq_ref, phase_ref, feats_ref, held_ref, sent_ref, local_ref, rows_ref):
    step = pl.program_id(0)
    out, core, chip = place_of_device()
    block = points_ref.shape[0]
    own = feats_ref.shape[1]
    n_out = freq_ref.shape[1] // own
    shard_rows = held_ref.shape[0]
    minibatch = index_ref.shape[1]

    @pl.when(step == 0)
    def _():
        base = (chip * 2 + core) * shard_rows
        index = index_ref[...]
        key = index * minibatch + lax.broadcasted_iota(jnp.int32, index.shape, 1)
        key_column = jnp.transpose(jnp.broadcast_to(key, (8, minibatch)))[:, :1]
        rank = jnp.sum((key_column < key).astype(jnp.int32), 0, keepdims=True)
        before = jnp.sum((index < base).astype(jnp.int32), 1, keepdims=True)
        first = (before - out + (n_out - 1)) // n_out
        inside = (index >= base) & (index < base + shard_rows) & (lax.rem(rank - out + n_out, n_out) == 0)
        slot = jnp.where(inside, (rank - out) // n_out - first, -1)
        here = slot == lax.broadcasted_iota(jnp.int32, (2 * SLOTS, minibatch), 0)
        local = jnp.sum(jnp.where(here, index - base + 1, 0), 1, keepdims=True) - 1
        local_ref[...] = jnp.broadcast_to(local, local_ref.shape)
        rows_ref[...] = jnp.zeros_like(rows_ref)

    points = points_ref[...]
    at = pl.multiple_of(out * own, own)
    phase = phase_ref[:, pl.ds(at, own)] * (0.5 / math.pi)
    turns = dot(points, freq_ref[:, pl.ds(at, own)]) * (0.5 / math.pi) + phase
    feats = cos_turns(turns, math.sqrt(2.0 / freq_ref.shape[1])).astype(BF16)
    feats_ref[...] = feats
    held_ref[pl.ds(pl.multiple_of(step * block, block), block), :] = feats
    columns = lax.broadcasted_iota(jnp.int32, (2 * SLOTS, block), 1)
    rows_ref[...] += dot((local_ref[:, :1] - step * block == columns).astype(F32).astype(BF16), points)

    @pl.when(step == pl.num_programs(0) - 1)
    def _():
        half = rows_ref.shape[1] // 2
        rows = rows_ref[...]
        sent_ref[...] = jnp.concatenate([rows[:SLOTS, :half], rows[:SLOTS, half:]], 0).astype(BF16)


def project_kernel(n_out, *refs):
    weight_refs, (feats_ref, sent_ref, pack_ref) = refs[:n_out], refs[n_out:]
    total = dot(jnp.concatenate([ref[...] for ref in weight_refs], 0), feats_ref[...])
    across = total.shape[1] // 128
    for at in range(pack_ref.shape[0]):
        r, c = divmod(at, across)
        high, low = split(total[8 * r : 8 * r + 8, 128 * c : 128 * c + 128])
        pack_ref[at, :16] = sent_ref[...]
        pack_ref[at, 16:] = jnp.concatenate([high.astype(F32), low.astype(F32)], 0).astype(BF16)


def gram_kernel(n_out, direct, *refs):
    weight_refs = refs[:n_out]
    at_ref, own_ref, other_ref, points_ref, norm_ref = refs[n_out : n_out + 5]
    kern_ref, kept_ref, given_ref, tile_ref, rows_ref, row_norm_ref, sum_ref = refs[n_out + 5 :]
    step = pl.program_id(0)

    @pl.when(step == 0)
    def _():
        peers, height, lanes = own_ref.shape
        if direct:
            rows = at_ref[...].astype(F32)
        else:
            columns = lax.broadcasted_iota(jnp.int32, (rows_ref.shape[0], peers * height), 1)
            halves = []
            for half in range(2):
                part = 0.0
                for source, held in enumerate((own_ref, other_ref)):
                    pick = (at_ref[source][:, :1] + half * SLOTS == columns).astype(F32).astype(BF16)
                    part = part + dot(pick, held[...].reshape(peers * height, lanes))
                halves.append(part)
            rows = jnp.concatenate(halves, 1)
        rows_ref[...] = rows.astype(BF16)
        row_norm_ref[...] = jnp.broadcast_to(jnp.sum(rows * rows, 1, keepdims=True), row_norm_ref.shape)
        sum_ref[...] = jnp.zeros_like(sum_ref)
        tile = jnp.sum(own_ref[:, 16:].astype(F32), 0) + jnp.sum(other_ref[:, 16:].astype(F32), 0)
        tile_ref[...] = tile[:8] + tile[8:]

    total = 0.0
    for at in range(0, points_ref.shape[0], CHUNK):
        here = pl.ds(at, CHUNK)
        inner = dot_nt(rows_ref[...], points_ref[here, :])
        squared = row_norm_ref[:, :1] + norm_ref[:, here] - 2.0 * inner
        scaled_square = (5.0 / (LENGTH * LENGTH)) * jnp.maximum(squared, 0.0)
        scaled_r = scaled_square * lax.rsqrt(jnp.maximum(scaled_square, 1e-30))
        kern = (1.0 + scaled_r + scaled_square * (1.0 / 3.0)) * jnp.exp(-scaled_r)
        kern = kern.astype(BF16)
        kern_ref[:, here] = kern
        weights = jnp.concatenate([ref[:, here] for ref in weight_refs], 0)
        total = total + dot_nt(weights, kern)
    sum_ref[...] += total

    @pl.when(step == pl.num_programs(0) - 1)
    def _():
        half = kept_ref.shape[0]
        core = lax.axis_index("core")
        lower, upper = sum_ref[:half], sum_ref[half:]
        kept_ref[...] = jnp.where(core == 0, lower, upper)
        given_ref[...] = jnp.where(core == 0, upper, lower)


def step_kernel(n_out, ratio, *refs):
    coregion_ref, noise_ref, targets_ref, own_ref, other_ref, feats_ref, kern_ref = refs[:7]
    base_ref, part_refs, (mixed_ref, weighted_ref) = refs[7], refs[8 : 7 + n_out], refs[7 + n_out :]
    draws = base_ref.shape[0]
    half = n_out * draws // 2

    @pl.when(pl.program_id(0) == 0)
    def _():
        out, core, _ = place_of_device()
        order = [lax.rem(out - k + n_out, n_out) for k in range(n_out)]
        mixer = [[coregion_ref[a, b] for b in order] for a in order]

        def mix(values):
            return [sum(c * v for c, v in zip(line, values)) for line in mixer]

        got = [own_ref[p].astype(F32) for p in range(own_ref.shape[0])]
        own = sum(block[:half] for block in got)
        other = sum(other_ref[p].astype(F32)[:half] for p in range(other_ref.shape[0]))
        total = jnp.concatenate([jnp.where(core == 0, own, other), jnp.where(core == 0, other, own)], 0)
        fitted = mix([total[draws * k : draws * (k + 1)] for k in range(n_out)])
        scaled = [
            (fitted[k] - targets_ref[draws * k : draws * (k + 1)]) / noise_ref[order[k]] for k in range(n_out)
        ]
        weighted = jnp.concatenate(mix(scaled), 0).astype(BF16)
        weighted_ref[...] = (weighted.astype(F32) * ratio).astype(BF16)
        across = mixed_ref.shape[1] // 128
        tiles = [block[half:] for block in got]
        lines = [
            jnp.concatenate(tiles[across * r : across * (r + 1)], 1) for r in range(n_out * draws // 8)
        ]
        each = draws // 8
        projected = [jnp.concatenate(lines[each * k : each * (k + 1)], 0) for k in range(n_out)]
        mixed_ref[...] = jnp.concatenate(mix(projected), 0).astype(BF16)

    gradient = dot(weighted_ref[...], kern_ref[...]) + dot_nt(mixed_ref[...], feats_ref[...])
    change = -STEP_SIZE * gradient
    base_ref[...] = change[:draws]
    for k, ref in enumerate(part_refs, 1):
        ref[...] = change[draws * k : draws * (k + 1)].astype(BF16)


def in_hbm(value):
    return pltpu.with_memory_space_constraint(value, pltpu.HBM)


def far_first(n_out):
    return sorted(range(1, n_out), key=lambda k: -min(k, n_out - k))


def swap_core(value):
    return lax.ppermute(value, "core", [(0, 1), (1, 0)])


def params(limit=None):
    return pltpu.CompilerParams(dimension_semantics=("arbitrary",), vmem_limit_bytes=limit)


def shards(points, rep_weights, batch_index, targets, noise_var, coregion, frequencies, phases):
    highest = lax.Precision.HIGHEST
    n_out = lax.axis_size("out")
    n_chips = lax.axis_size("z") * lax.axis_size("y")
    n_pts = 2 * n_chips
    rows, width = points.shape
    draws = rep_weights.shape[2]
    minibatch = batch_index.shape[0]
    own_rows = minibatch // n_out
    own_features = frequencies.shape[1] // n_out
    cols = n_out * draws
    out, core, chip = place_of_device()
    shard = chip * 2 + core
    ratio = (rows * n_pts) / minibatch

    own_weights = rep_weights[0].T
    low = own_weights.astype(BF16)
    weights = [low] * n_out
    for k in far_first(n_out):
        weights[k] = lax.ppermute(low, "out", [(i, (i + k) % n_out) for i in range(n_out)])
    weight_specs = lambda block: [pl.BlockSpec((draws, block), lambda i: (0, i))] * n_out
    point_spec = lambda block: pl.BlockSpec((block, width), lambda i: (i, 0))
    feat_spec = lambda block: pl.BlockSpec((block, own_features), lambda i: (i, 0))
    kern_spec = lambda block: pl.BlockSpec((own_rows, block), lambda i: (0, i))
    draw_spec = lambda block: pl.BlockSpec((draws, block), lambda i: (0, i))

    feats, held, sent_rows = pl.pallas_call(
        features_kernel,
        grid=(rows // FEATURES_BLOCK,),
        out_shape=(
            pltpu.HBM((rows, own_features), BF16),
            pltpu.VMEM((rows, own_features), BF16),
            jax.ShapeDtypeStruct((2 * SLOTS, width // 2), BF16),
        ),
        in_specs=[
            whole((1, minibatch)),
            point_spec(FEATURES_BLOCK),
            whole(frequencies.shape),
            whole((1, phases.shape[0])),
        ],
        out_specs=(
            feat_spec(FEATURES_BLOCK),
            pl.BlockSpec(memory_space=pltpu.VMEM),
            whole((2 * SLOTS, width // 2)),
        ),
        scratch_shapes=[pltpu.VMEM((2 * SLOTS, 128), jnp.int32), pltpu.VMEM((2 * SLOTS, width), F32)],
        compiler_params=params(SMALL_VMEM),
        name="features",
    )(in_hbm(batch_index[None]), in_hbm(points), in_hbm(frequencies), in_hbm(phases[None]))

    in_vmem = pl.BlockSpec(memory_space=pltpu.VMEM)
    pack = pl.pallas_call(
        functools.partial(project_kernel, n_out),
        out_shape=jax.ShapeDtypeStruct((n_chips, 32, 128), BF16),
        in_specs=[in_vmem] * (n_out + 2),
        out_specs=in_vmem,
        compiler_params=pltpu.CompilerParams(vmem_limit_bytes=SMALL_VMEM),
        name="project",
    )(*weights, pltpu.with_memory_space_constraint(held, pltpu.VMEM), sent_rows)
    got = lax.all_to_all(pack, CHIP_AXES, 0, 0)
    batch_index, points_now, targets, _ = lax.optimization_barrier((batch_index, points, targets, pack))

    key = batch_index * minibatch + lax.iota(jnp.int32, minibatch)
    rank = jnp.sum((key[None, :] < key[:, None]).astype(jnp.int32), 1)
    own_rank = lax.iota(jnp.int32, own_rows) * n_out + out
    chosen = own_rank[:, None] == rank[None, :]
    own_index = jnp.sum(jnp.where(chosen, batch_index[None, :], 0), 1)
    own_shard = own_index // rows
    starts = jnp.sum((own_index[None, :] < (own_shard * rows)[:, None]).astype(jnp.int32), 1)
    slot = lax.iota(jnp.int32, own_rows) - starts
    same_shard = (batch_index // rows)[None, :] == (batch_index // rows)[:, None]
    most = jnp.max(jnp.sum(same_shard.astype(jnp.int32), 1))
    overflow = most > SLOTS * n_out
    at = (own_shard // 2) * 32 + slot
    own_core = (own_shard % 2) == core
    at = jnp.stack([jnp.where(own_core, at, -64), jnp.where(own_core, -64, at)])
    at = jnp.broadcast_to(at[:, :, None], (2, own_rows, 128))
    col_norm = jnp.sum(jnp.square(points_now.astype(F32)), 1)[None]
    order = lax.rem(out - lax.iota(jnp.int32, n_out) + n_out, n_out)
    own_targets = jnp.einsum("im,qms->qsi", chosen.astype(F32), targets, precision=highest)[order]
    own_targets = own_targets.reshape(cols, own_rows)
    got, at, overflow, own_index, col_norm, own_targets = lax.optimization_barrier(
        (got, at, overflow, own_index, col_norm, own_targets)
    )
    got_other = swap_core(got)

    def gram(direct, where):
        return pl.pallas_call(
            functools.partial(gram_kernel, n_out, direct),
            grid=(1,),
            out_shape=(
                jax.ShapeDtypeStruct((own_rows, rows), BF16),
                jax.ShapeDtypeStruct((cols // 2, own_rows), F32),
                jax.ShapeDtypeStruct((cols // 2, own_rows), F32),
                jax.ShapeDtypeStruct((8, 128), F32),
            ),
            in_specs=[pl.BlockSpec(memory_space=pltpu.VMEM)] * (n_out + 5),
            out_specs=(
                pl.BlockSpec(memory_space=pltpu.VMEM),
                pl.BlockSpec(memory_space=pltpu.VMEM),
                pl.BlockSpec(memory_space=pltpu.VMEM),
                pl.BlockSpec(memory_space=pltpu.VMEM),
            ),
            scratch_shapes=[
                pltpu.VMEM((own_rows, width), BF16),
                pltpu.VMEM((own_rows, 128), F32),
                pltpu.VMEM((cols, own_rows), F32),
            ],
            compiler_params=params(SMALL_VMEM),
            name="gram_fetched" if direct else "gram",
        )(*weights, where, got, got_other, pltpu.with_memory_space_constraint(points, pltpu.VMEM), col_norm)

    def fetch():
        local = own_index - shard * rows
        inside = (local >= 0) & (local < rows)
        picked = jnp.where(inside[:, None], points[jnp.clip(local, 0, rows - 1)].astype(F32), 0.0)
        return gram(True, lax.psum(picked, POINT_AXES).astype(BF16))

    kern, kept, given, tile = lax.cond(overflow, fetch, lambda: gram(False, at))

    pack = jnp.concatenate([kept + swap_core(given), tile], 0).astype(BF16)
    pack = jnp.broadcast_to(pack[None], (n_chips, *pack.shape))
    got = lax.all_to_all(pack, CHIP_AXES, 0, 0)
    got_other = swap_core(got)

    base, *parts = pl.pallas_call(
        functools.partial(step_kernel, n_out, ratio),
        grid=(rows // STEP_BLOCK,),
        out_shape=[jax.ShapeDtypeStruct((draws, rows), F32)]
        + [jax.ShapeDtypeStruct((draws, rows), BF16)] * (n_out - 1),
        in_specs=[
            pl.BlockSpec(memory_space=pltpu.SMEM),
            pl.BlockSpec(memory_space=pltpu.SMEM),
            whole(own_targets.shape),
            whole(got.shape),
            whole(got.shape),
            feat_spec(STEP_BLOCK),
            kern_spec(STEP_BLOCK),
        ],
        out_specs=[draw_spec(STEP_BLOCK)] * n_out,
        scratch_shapes=[pltpu.VMEM((cols, own_features), BF16), pltpu.VMEM((cols, own_rows), BF16)],
        compiler_params=params(SMALL_VMEM),
        name="step",
    )(coregion, noise_var, own_targets, got, got_other, in_hbm(feats), in_hbm(kern))
    total = own_weights + base
    for k in far_first(n_out):
        part = lax.ppermute(parts[k - 1], "out", [(i, (i - k) % n_out) for i in range(n_out)])
        total = total + part.astype(F32)
    return total.T[None]


def solution(mesh):
    fine = Mesh(mesh.devices.reshape(8, 4, 2, 4), ("z", "y", "core", "out"))
    in_specs = (P(POINT_AXES, None), P("out", POINT_AXES, None), P(), P(), P(), P(), P(), P())
    out_specs = P("out", POINT_AXES, None)
    return jax.shard_map(shards, mesh=fine, in_specs=in_specs, out_specs=out_specs, check_vma=False)
```

```python
import functools
import math

import jax
import jax.numpy as jnp
from jax import lax
from jax.experimental import pallas as pl
from jax.experimental.pallas import tpu as pltpu
from jax.sharding import Mesh
from jax.sharding import PartitionSpec as P

LENGTH = 0.5
STEP_SIZE = 0.5
SLOTS = 8
CHUNK = 1024
FEATURES_BLOCK = 2048
STEP_BLOCK = 2048
SMALL_VMEM = 24 * 1024 * 1024
SIN_TURNS = (
    6.283185160088695,
    -41.34165503124932,
    81.60100406363227,
    -76.54978208799582,
    39.53670460277009,
)
POINT_AXES = ("z", "y", "core")
ROOT = (4, 2)
BF16 = jnp.bfloat16
F32 = jnp.float32
NT = (((1,), (1,)), ((), ()))


def dot(a, b):
    return jnp.dot(a, b, preferred_element_type=F32)


def dot_nt(a, b):
    return lax.dot_general(a, b, NT, preferred_element_type=F32)


def cos_turns(turns, scale):
    rest = turns - jnp.round(turns)
    quarter = 0.25 - jnp.abs(rest)
    square = quarter * quarter
    poly = F32(SIN_TURNS[-1] * scale)
    for coefficient in SIN_TURNS[-2::-1]:
        poly = poly * square + F32(coefficient * scale)
    return poly * quarter


def split(value):
    high = value.astype(BF16)
    return high, (value - high.astype(F32)).astype(BF16)


def place_of_device():
    chip = lax.axis_index("z") * lax.axis_size("y") + lax.axis_index("y")
    return lax.axis_index("out"), lax.axis_index("core"), chip


def whole(shape):
    return pl.BlockSpec(shape, lambda i: (0,) * len(shape))


def features_of(points, freq_ref, phase_ref, at, own):
    phase = phase_ref[:, pl.ds(at, own)] * (0.5 / math.pi)
    turns = dot(points, freq_ref[:, pl.ds(at, own)]) * (0.5 / math.pi) + phase
    return cos_turns(turns, math.sqrt(2.0 / freq_ref.shape[1])).astype(BF16)


def picked_rows(local, first, points):
    columns = lax.broadcasted_iota(jnp.int32, (2 * SLOTS, points.shape[0]), 1)
    return dot((local[:, :1] - first == columns).astype(F32).astype(BF16), points)


def features_kernel(index_ref, points_ref, freq_ref, phase_ref, feats_ref, held_ref, sent_ref, local_ref, rows_ref):
    step = pl.program_id(0)
    out, core, chip = place_of_device()
    block = points_ref.shape[0]
    own = feats_ref.shape[1]
    n_out = freq_ref.shape[1] // own
    shard_rows = held_ref.shape[0]
    minibatch = index_ref.shape[1]

    @pl.when(step == 0)
    def _():
        base = (chip * 2 + core) * shard_rows
        index = index_ref[...]
        key = index * minibatch + lax.broadcasted_iota(jnp.int32, index.shape, 1)
        key_column = jnp.transpose(jnp.broadcast_to(key, (8, minibatch)))[:, :1]
        rank = jnp.sum((key_column < key).astype(jnp.int32), 0, keepdims=True)
        before = jnp.sum((index < base).astype(jnp.int32), 1, keepdims=True)
        first = (before - out + (n_out - 1)) // n_out
        inside = (index >= base) & (index < base + shard_rows) & (lax.rem(rank - out + n_out, n_out) == 0)
        slot = jnp.where(inside, (rank - out) // n_out - first, -1)
        here = slot == lax.broadcasted_iota(jnp.int32, (2 * SLOTS, minibatch), 0)
        local = jnp.sum(jnp.where(here, index - base + 1, 0), 1, keepdims=True) - 1
        local_ref[...] = jnp.broadcast_to(local, local_ref.shape)
        rows_ref[...] = jnp.zeros_like(rows_ref)

    points = points_ref[...]
    at = pl.multiple_of(out * own, own)
    phase = phase_ref[:, pl.ds(at, own)] * (0.5 / math.pi)
    turns = dot(points, freq_ref[:, pl.ds(at, own)]) * (0.5 / math.pi) + phase
    feats = cos_turns(turns, math.sqrt(2.0 / freq_ref.shape[1])).astype(BF16)
    feats_ref[...] = feats
    held_ref[pl.ds(pl.multiple_of(step * block, block), block), :] = feats
    columns = lax.broadcasted_iota(jnp.int32, (2 * SLOTS, block), 1)
    rows_ref[...] += dot((local_ref[:, :1] - step * block == columns).astype(F32).astype(BF16), points)

    @pl.when(step == pl.num_programs(0) - 1)
    def _():
        half = rows_ref.shape[1] // 2
        rows = rows_ref[...]
        sent_ref[...] = jnp.concatenate([rows[:SLOTS, :half], rows[:SLOTS, half:]], 0).astype(BF16)


def project_kernel(n_out, *refs):
    weight_refs, (feats_ref, sent_ref, pack_ref) = refs[:n_out], refs[n_out:]
    total = dot(jnp.concatenate([ref[...] for ref in weight_refs], 0), feats_ref[...])
    across = total.shape[1] // 128
    for at in range(pack_ref.shape[0]):
        r, c = divmod(at, across)
        high, low = split(total[8 * r : 8 * r + 8, 128 * c : 128 * c + 128])
        pack_ref[at, :16] = sent_ref[...]
        pack_ref[at, 16:] = jnp.concatenate([high.astype(F32), low.astype(F32)], 0).astype(BF16)


def gram_kernel(n_out, direct, *refs):
    weight_refs = refs[:n_out]
    at_ref, own_ref, other_ref, points_ref, norm_ref = refs[n_out : n_out + 5]
    kern_ref, kept_ref, given_ref, tile_ref, rows_ref, row_norm_ref, sum_ref = refs[n_out + 5 :]
    step = pl.program_id(0)

    @pl.when(step == 0)
    def _():
        peers, height, lanes = own_ref.shape
        if direct:
            rows = at_ref[...].astype(F32)
        else:
            columns = lax.broadcasted_iota(jnp.int32, (rows_ref.shape[0], peers * height), 1)
            halves = []
            for half in range(2):
                part = 0.0
                for source, held in enumerate((own_ref, other_ref)):
                    pick = (at_ref[source][:, :1] + half * SLOTS == columns).astype(F32).astype(BF16)
                    part = part + dot(pick, held[...].reshape(peers * height, lanes))
                halves.append(part)
            rows = jnp.concatenate(halves, 1)
        rows_ref[...] = rows.astype(BF16)
        row_norm_ref[...] = jnp.broadcast_to(jnp.sum(rows * rows, 1, keepdims=True), row_norm_ref.shape)
        sum_ref[...] = jnp.zeros_like(sum_ref)
        tile = jnp.sum(own_ref[:, 16:].astype(F32), 0) + jnp.sum(other_ref[:, 16:].astype(F32), 0)
        tile_ref[...] = tile[:8] + tile[8:]

    total = 0.0
    for at in range(0, points_ref.shape[0], CHUNK):
        here = pl.ds(at, CHUNK)
        inner = dot_nt(rows_ref[...], points_ref[here, :])
        squared = row_norm_ref[:, :1] + norm_ref[:, here] - 2.0 * inner
        scaled_square = (5.0 / (LENGTH * LENGTH)) * jnp.maximum(squared, 0.0)
        scaled_r = scaled_square * lax.rsqrt(jnp.maximum(scaled_square, 1e-30))
        kern = (1.0 + scaled_r + scaled_square * (1.0 / 3.0)) * jnp.exp(-scaled_r)
        kern = kern.astype(BF16)
        kern_ref[:, here] = kern
        weights = jnp.concatenate([ref[:, here] for ref in weight_refs], 0)
        total = total + dot_nt(weights, kern)
    sum_ref[...] += total

    @pl.when(step == pl.num_programs(0) - 1)
    def _():
        half = kept_ref.shape[0]
        core = lax.axis_index("core")
        lower, upper = sum_ref[:half], sum_ref[half:]
        kept_ref[...] = jnp.where(core == 0, lower, upper)
        given_ref[...] = jnp.where(core == 0, upper, lower)


def step_kernel(n_out, ratio, *refs):
    coregion_ref, noise_ref, targets_ref, own_ref, other_ref, feats_ref, kern_ref = refs[:7]
    base_ref, part_refs, (mixed_ref, weighted_ref) = refs[7], refs[8 : 7 + n_out], refs[7 + n_out :]
    draws = base_ref.shape[0]
    half = n_out * draws // 2

    @pl.when(pl.program_id(0) == 0)
    def _():
        out, core, _ = place_of_device()
        order = [lax.rem(out - k + n_out, n_out) for k in range(n_out)]
        mixer = [[coregion_ref[a, b] for b in order] for a in order]

        def mix(values):
            return [sum(c * v for c, v in zip(line, values)) for line in mixer]

        got = [own_ref[p].astype(F32) for p in range(own_ref.shape[0])]
        own = sum(block[:half] for block in got)
        other = sum(other_ref[p].astype(F32)[:half] for p in range(other_ref.shape[0]))
        total = jnp.concatenate([jnp.where(core == 0, own, other), jnp.where(core == 0, other, own)], 0)
        fitted = mix([total[draws * k : draws * (k + 1)] for k in range(n_out)])
        scaled = [
            (fitted[k] - targets_ref[draws * k : draws * (k + 1)]) / noise_ref[order[k]] for k in range(n_out)
        ]
        weighted = jnp.concatenate(mix(scaled), 0).astype(BF16)
        weighted_ref[...] = (weighted.astype(F32) * ratio).astype(BF16)
        across = mixed_ref.shape[1] // 128
        tiles = [block[half:] for block in got]
        lines = [
            jnp.concatenate(tiles[across * r : across * (r + 1)], 1) for r in range(n_out * draws // 8)
        ]
        each = draws // 8
        projected = [jnp.concatenate(lines[each * k : each * (k + 1)], 0) for k in range(n_out)]
        mixed_ref[...] = jnp.concatenate(mix(projected), 0).astype(BF16)

    gradient = dot(weighted_ref[...], kern_ref[...]) + dot_nt(mixed_ref[...], feats_ref[...])
    change = -STEP_SIZE * gradient
    base_ref[...] = change[:draws]
    for k, ref in enumerate(part_refs, 1):
        ref[...] = change[draws * k : draws * (k + 1)].astype(BF16)


def in_hbm(value):
    return pltpu.with_memory_space_constraint(value, pltpu.HBM)


def exchange(value):
    z, y = lax.axis_size("z"), lax.axis_size("y")
    order = [((ROOT[0] + a) % z) * y + (ROOT[1] + b) % y for a in range(z) for b in range(y)]
    groups = [[2 * chip + core for chip in order] for core in range(2)]
    return lax.all_to_all(value, POINT_AXES, 0, 0, axis_index_groups=groups)


def far_first(n_out):
    return sorted(range(1, n_out), key=lambda k: -min(k, n_out - k))


def swap_core(value):
    return lax.ppermute(value, "core", [(0, 1), (1, 0)])


def params(limit=None):
    return pltpu.CompilerParams(dimension_semantics=("arbitrary",), vmem_limit_bytes=limit)


def shards(points, rep_weights, batch_index, targets, noise_var, coregion, frequencies, phases):
    highest = lax.Precision.HIGHEST
    n_out = lax.axis_size("out")
    n_chips = lax.axis_size("z") * lax.axis_size("y")
    n_pts = 2 * n_chips
    rows, width = points.shape
    draws = rep_weights.shape[2]
    minibatch = batch_index.shape[0]
    own_rows = minibatch // n_out
    own_features = frequencies.shape[1] // n_out
    cols = n_out * draws
    out, core, chip = place_of_device()
    shard = chip * 2 + core
    ratio = (rows * n_pts) / minibatch

    own_weights = rep_weights[0].T
    low = own_weights.astype(BF16)
    weights = [low] * n_out
    for k in far_first(n_out):
        weights[k] = lax.ppermute(low, "out", [(i, (i + k) % n_out) for i in range(n_out)])
    weight_specs = lambda block: [pl.BlockSpec((draws, block), lambda i: (0, i))] * n_out
    point_spec = lambda block: pl.BlockSpec((block, width), lambda i: (i, 0))
    feat_spec = lambda block: pl.BlockSpec((block, own_features), lambda i: (i, 0))
    kern_spec = lambda block: pl.BlockSpec((own_rows, block), lambda i: (0, i))
    draw_spec = lambda block: pl.BlockSpec((draws, block), lambda i: (0, i))

    feats, held, sent_rows = pl.pallas_call(
        features_kernel,
        grid=(rows // FEATURES_BLOCK,),
        out_shape=(
            pltpu.HBM((rows, own_features), BF16),
            pltpu.VMEM((rows, own_features), BF16),
            jax.ShapeDtypeStruct((2 * SLOTS, width // 2), BF16),
        ),
        in_specs=[
            whole((1, minibatch)),
            point_spec(FEATURES_BLOCK),
            whole(frequencies.shape),
            whole((1, phases.shape[0])),
        ],
        out_specs=(
            feat_spec(FEATURES_BLOCK),
            pl.BlockSpec(memory_space=pltpu.VMEM),
            whole((2 * SLOTS, width // 2)),
        ),
        scratch_shapes=[pltpu.VMEM((2 * SLOTS, 128), jnp.int32), pltpu.VMEM((2 * SLOTS, width), F32)],
        compiler_params=params(SMALL_VMEM),
        name="features",
    )(in_hbm(batch_index[None]), in_hbm(points), in_hbm(frequencies), in_hbm(phases[None]))

    in_vmem = pl.BlockSpec(memory_space=pltpu.VMEM)
    pack = pl.pallas_call(
        functools.partial(project_kernel, n_out),
        out_shape=jax.ShapeDtypeStruct((n_chips, 32, 128), BF16),
        in_specs=[in_vmem] * (n_out + 2),
        out_specs=in_vmem,
        compiler_params=pltpu.CompilerParams(vmem_limit_bytes=SMALL_VMEM),
        name="project",
    )(*weights, pltpu.with_memory_space_constraint(held, pltpu.VMEM), sent_rows)
    got = exchange(pack)
    batch_index, points_now, targets, _ = lax.optimization_barrier((batch_index, points, targets, pack))

    key = batch_index * minibatch + lax.iota(jnp.int32, minibatch)
    rank = jnp.sum((key[None, :] < key[:, None]).astype(jnp.int32), 1)
    own_rank = lax.iota(jnp.int32, own_rows) * n_out + out
    chosen = own_rank[:, None] == rank[None, :]
    own_index = jnp.sum(jnp.where(chosen, batch_index[None, :], 0), 1)
    own_shard = own_index // rows
    starts = jnp.sum((own_index[None, :] < (own_shard * rows)[:, None]).astype(jnp.int32), 1)
    slot = lax.iota(jnp.int32, own_rows) - starts
    same_shard = (batch_index // rows)[None, :] == (batch_index // rows)[:, None]
    most = jnp.max(jnp.sum(same_shard.astype(jnp.int32), 1))
    overflow = most > SLOTS * n_out
    own_chip = own_shard // 2
    n_y = lax.axis_size("y")
    block = (own_chip // n_y - ROOT[0]) % lax.axis_size("z") * n_y + (own_chip - ROOT[1]) % n_y
    at = block * 32 + slot
    own_core = (own_shard % 2) == core
    at = jnp.stack([jnp.where(own_core, at, -64), jnp.where(own_core, -64, at)])
    at = jnp.broadcast_to(at[:, :, None], (2, own_rows, 128))
    col_norm = jnp.sum(jnp.square(points_now.astype(F32)), 1)[None]
    order = lax.rem(out - lax.iota(jnp.int32, n_out) + n_out, n_out)
    own_targets = jnp.einsum("im,qms->qsi", chosen.astype(F32), targets, precision=highest)[order]
    own_targets = own_targets.reshape(cols, own_rows)
    got, at, overflow, own_index, col_norm, own_targets = lax.optimization_barrier(
        (got, at, overflow, own_index, col_norm, own_targets)
    )
    got_other = swap_core(got)

    def gram(direct, where):
        return pl.pallas_call(
            functools.partial(gram_kernel, n_out, direct),
            grid=(1,),
            out_shape=(
                jax.ShapeDtypeStruct((own_rows, rows), BF16),
                jax.ShapeDtypeStruct((cols // 2, own_rows), F32),
                jax.ShapeDtypeStruct((cols // 2, own_rows), F32),
                jax.ShapeDtypeStruct((8, 128), F32),
            ),
            in_specs=[pl.BlockSpec(memory_space=pltpu.VMEM)] * (n_out + 5),
            out_specs=(
                pl.BlockSpec(memory_space=pltpu.VMEM),
                pl.BlockSpec(memory_space=pltpu.VMEM),
                pl.BlockSpec(memory_space=pltpu.VMEM),
                pl.BlockSpec(memory_space=pltpu.VMEM),
            ),
            scratch_shapes=[
                pltpu.VMEM((own_rows, width), BF16),
                pltpu.VMEM((own_rows, 128), F32),
                pltpu.VMEM((cols, own_rows), F32),
            ],
            compiler_params=params(SMALL_VMEM),
            name="gram_fetched" if direct else "gram",
        )(*weights, where, got, got_other, pltpu.with_memory_space_constraint(points, pltpu.VMEM), col_norm)

    def fetch():
        local = own_index - shard * rows
        inside = (local >= 0) & (local < rows)
        picked = jnp.where(inside[:, None], points[jnp.clip(local, 0, rows - 1)].astype(F32), 0.0)
        return gram(True, lax.psum(picked, POINT_AXES).astype(BF16))

    kern, kept, given, tile = lax.cond(overflow, fetch, lambda: gram(False, at))

    pack = jnp.concatenate([kept + swap_core(given), tile], 0).astype(BF16)
    pack = jnp.broadcast_to(pack[None], (n_chips, *pack.shape))
    got = exchange(pack)
    got_other = swap_core(got)

    base, *parts = pl.pallas_call(
        functools.partial(step_kernel, n_out, ratio),
        grid=(rows // STEP_BLOCK,),
        out_shape=[jax.ShapeDtypeStruct((draws, rows), F32)]
        + [jax.ShapeDtypeStruct((draws, rows), BF16)] * (n_out - 1),
        in_specs=[
            pl.BlockSpec(memory_space=pltpu.SMEM),
            pl.BlockSpec(memory_space=pltpu.SMEM),
            whole(own_targets.shape),
            whole(got.shape),
            whole(got.shape),
            feat_spec(STEP_BLOCK),
            kern_spec(STEP_BLOCK),
        ],
        out_specs=[draw_spec(STEP_BLOCK)] * n_out,
        scratch_shapes=[pltpu.VMEM((cols, own_features), BF16), pltpu.VMEM((cols, own_rows), BF16)],
        compiler_params=params(SMALL_VMEM),
        name="step",
    )(coregion, noise_var, own_targets, got, got_other, in_hbm(feats), in_hbm(kern))
    total = own_weights + base
    for k in far_first(n_out):
        part = lax.ppermute(parts[k - 1], "out", [(i, (i - k) % n_out) for i in range(n_out)])
        total = total + part.astype(F32)
    return total.T[None]


def solution(mesh):
    fine = Mesh(mesh.devices.reshape(8, 4, 2, 4), ("z", "y", "core", "out"))
    in_specs = (P(POINT_AXES, None), P("out", POINT_AXES, None), P(), P(), P(), P(), P(), P())
    out_specs = P("out", POINT_AXES, None)
    return jax.shard_map(shards, mesh=fine, in_specs=in_specs, out_specs=out_specs, check_vma=False)
```

```python
import functools
import math

import jax
import jax.numpy as jnp
from jax import lax
from jax.experimental import pallas as pl
from jax.experimental.pallas import tpu as pltpu
from jax.sharding import Mesh
from jax.sharding import PartitionSpec as P

LENGTH = 0.5
STEP_SIZE = 0.5
SLOTS = 8
CHUNK = 1024
FEATURES_BLOCK = 2048
STEP_BLOCK = 2048
SMALL_VMEM = 24 * 1024 * 1024
SIN_TURNS = (
    6.283185160088695,
    -41.34165503124932,
    81.60100406363227,
    -76.54978208799582,
    39.53670460277009,
)
POINT_AXES = ("z", "y", "core")
ROOT = (4, 2)
BF16 = jnp.bfloat16
F32 = jnp.float32
NT = (((1,), (1,)), ((), ()))


def dot(a, b):
    return jnp.dot(a, b, preferred_element_type=F32)


def dot_nt(a, b):
    return lax.dot_general(a, b, NT, preferred_element_type=F32)


def cos_turns(turns, scale):
    rest = turns - jnp.round(turns)
    quarter = 0.25 - jnp.abs(rest)
    square = quarter * quarter
    poly = F32(SIN_TURNS[-1] * scale)
    for coefficient in SIN_TURNS[-2::-1]:
        poly = poly * square + F32(coefficient * scale)
    return poly * quarter


def split(value):
    high = value.astype(BF16)
    return high, (value - high.astype(F32)).astype(BF16)


def place_of_device():
    chip = lax.axis_index("z") * lax.axis_size("y") + lax.axis_index("y")
    return lax.axis_index("out"), lax.axis_index("core"), chip


def whole(shape):
    return pl.BlockSpec(shape, lambda i: (0,) * len(shape))


def features_of(points, freq_ref, phase_ref, at, own):
    phase = phase_ref[:, pl.ds(at, own)] * (0.5 / math.pi)
    turns = dot(points, freq_ref[:, pl.ds(at, own)]) * (0.5 / math.pi) + phase
    return cos_turns(turns, math.sqrt(2.0 / freq_ref.shape[1])).astype(BF16)


def picked_rows(local, first, points):
    columns = lax.broadcasted_iota(jnp.int32, (2 * SLOTS, points.shape[0]), 1)
    return dot((local[:, :1] - first == columns).astype(F32).astype(BF16), points)


def features_kernel(index_ref, points_ref, freq_ref, phase_ref, feats_ref, held_ref, sent_ref, local_ref, rows_ref):
    step = pl.program_id(0)
    out, core, chip = place_of_device()
    block = points_ref.shape[0]
    own = feats_ref.shape[1]
    n_out = freq_ref.shape[1] // own
    shard_rows = held_ref.shape[0]
    minibatch = index_ref.shape[1]

    @pl.when(step == 0)
    def _():
        base = (chip * 2 + core) * shard_rows
        index = index_ref[...]
        key = index * minibatch + lax.broadcasted_iota(jnp.int32, index.shape, 1)
        key_column = jnp.transpose(jnp.broadcast_to(key, (8, minibatch)))[:, :1]
        rank = jnp.sum((key_column < key).astype(jnp.int32), 0, keepdims=True)
        before = jnp.sum((index < base).astype(jnp.int32), 1, keepdims=True)
        first = (before - out + (n_out - 1)) // n_out
        inside = (index >= base) & (index < base + shard_rows) & (lax.rem(rank - out + n_out, n_out) == 0)
        slot = jnp.where(inside, (rank - out) // n_out - first, -1)
        here = slot == lax.broadcasted_iota(jnp.int32, (2 * SLOTS, minibatch), 0)
        local = jnp.sum(jnp.where(here, index - base + 1, 0), 1, keepdims=True) - 1
        local_ref[...] = jnp.broadcast_to(local, local_ref.shape)
        rows_ref[...] = jnp.zeros_like(rows_ref)

    points = points_ref[...]
    at = pl.multiple_of(out * own, own)
    phase = phase_ref[:, pl.ds(at, own)] * (0.5 / math.pi)
    turns = dot(points, freq_ref[:, pl.ds(at, own)]) * (0.5 / math.pi) + phase
    feats = cos_turns(turns, math.sqrt(2.0 / freq_ref.shape[1])).astype(BF16)
    feats_ref[...] = feats
    held_ref[pl.ds(pl.multiple_of(step * block, block), block), :] = feats
    columns = lax.broadcasted_iota(jnp.int32, (2 * SLOTS, block), 1)
    rows_ref[...] += dot((local_ref[:, :1] - step * block == columns).astype(F32).astype(BF16), points)

    @pl.when(step == pl.num_programs(0) - 1)
    def _():
        half = rows_ref.shape[1] // 2
        rows = rows_ref[...]
        sent_ref[...] = jnp.concatenate([rows[:SLOTS, :half], rows[:SLOTS, half:]], 0).astype(BF16)


def project_kernel(n_out, *refs):
    weight_refs, (feats_ref, sent_ref, pack_ref) = refs[:n_out], refs[n_out:]
    total = dot(jnp.concatenate([ref[...] for ref in weight_refs], 0), feats_ref[...])
    across = total.shape[1] // 128
    for at in range(pack_ref.shape[0]):
        r, c = divmod(at, across)
        high, low = split(total[8 * r : 8 * r + 8, 128 * c : 128 * c + 128])
        pack_ref[at, :16] = sent_ref[...]
        pack_ref[at, 16:] = jnp.concatenate([high.astype(F32), low.astype(F32)], 0).astype(BF16)


def gram_kernel(n_out, direct, *refs):
    weight_refs = refs[:n_out]
    at_ref, own_ref, other_ref, points_ref, norm_ref = refs[n_out : n_out + 5]
    kern_ref, kept_ref, given_ref, tile_ref, rows_ref, row_norm_ref, sum_ref = refs[n_out + 5 :]
    step = pl.program_id(0)

    @pl.when(step == 0)
    def _():
        peers, height, lanes = own_ref.shape
        if direct:
            rows = at_ref[...].astype(F32)
        else:
            columns = lax.broadcasted_iota(jnp.int32, (rows_ref.shape[0], peers * height), 1)
            halves = []
            for half in range(2):
                part = 0.0
                for source, held in enumerate((own_ref, other_ref)):
                    pick = (at_ref[source][:, :1] + half * SLOTS == columns).astype(F32).astype(BF16)
                    part = part + dot(pick, held[...].reshape(peers * height, lanes))
                halves.append(part)
            rows = jnp.concatenate(halves, 1)
        rows_ref[...] = rows.astype(BF16)
        row_norm_ref[...] = jnp.broadcast_to(jnp.sum(rows * rows, 1, keepdims=True), row_norm_ref.shape)
        sum_ref[...] = jnp.zeros_like(sum_ref)
        tile = jnp.sum(own_ref[:, 16:].astype(F32), 0) + jnp.sum(other_ref[:, 16:].astype(F32), 0)
        tile_ref[...] = tile[:8] + tile[8:]

    total = 0.0
    for at in range(0, points_ref.shape[0], CHUNK):
        here = pl.ds(at, CHUNK)
        inner = dot_nt(rows_ref[...], points_ref[here, :])
        squared = row_norm_ref[:, :1] + norm_ref[:, here] - 2.0 * inner
        scaled_square = (5.0 / (LENGTH * LENGTH)) * jnp.maximum(squared, 0.0)
        scaled_r = scaled_square * lax.rsqrt(jnp.maximum(scaled_square, 1e-30))
        kern = (1.0 + scaled_r + scaled_square * (1.0 / 3.0)) * jnp.exp(-scaled_r)
        kern = kern.astype(BF16)
        kern_ref[:, here] = kern
        weights = jnp.concatenate([ref[:, here] for ref in weight_refs], 0)
        total = total + dot_nt(weights, kern)
    sum_ref[...] += total

    @pl.when(step == pl.num_programs(0) - 1)
    def _():
        half = kept_ref.shape[0]
        core = lax.axis_index("core")
        lower, upper = sum_ref[:half], sum_ref[half:]
        kept_ref[...] = jnp.where(core == 0, lower, upper)
        given_ref[...] = jnp.where(core == 0, upper, lower)


def step_kernel(n_out, ratio, *refs):
    coregion_ref, noise_ref, targets_ref, own_ref, other_ref, feats_ref, kern_ref = refs[:7]
    base_ref, part_refs, (mixed_ref, weighted_ref) = refs[7], refs[8 : 7 + n_out], refs[7 + n_out :]
    draws = base_ref.shape[0]
    half = n_out * draws // 2

    @pl.when(pl.program_id(0) == 0)
    def _():
        out, core, _ = place_of_device()
        order = [lax.rem(out + k, n_out) for k in range(n_out)]
        mixer = [[coregion_ref[a, b] for b in order] for a in order]

        def mix(values):
            return [sum(c * v for c, v in zip(line, values)) for line in mixer]

        got = [own_ref[p].astype(F32) for p in range(own_ref.shape[0])]
        own = sum(block[:half] for block in got)
        other = sum(other_ref[p].astype(F32)[:half] for p in range(other_ref.shape[0]))
        total = jnp.concatenate([jnp.where(core == 0, own, other), jnp.where(core == 0, other, own)], 0)
        fitted = mix([total[draws * k : draws * (k + 1)] for k in range(n_out)])
        scaled = [
            (fitted[k] - targets_ref[draws * k : draws * (k + 1)]) / noise_ref[order[k]] for k in range(n_out)
        ]
        weighted = jnp.concatenate(mix(scaled), 0).astype(BF16)
        weighted_ref[...] = (weighted.astype(F32) * ratio).astype(BF16)
        across = mixed_ref.shape[1] // 128
        tiles = [block[half:] for block in got]
        lines = [
            jnp.concatenate(tiles[across * r : across * (r + 1)], 1) for r in range(n_out * draws // 8)
        ]
        each = draws // 8
        projected = [jnp.concatenate(lines[each * k : each * (k + 1)], 0) for k in range(n_out)]
        mixed_ref[...] = jnp.concatenate(mix(projected), 0).astype(BF16)

    gradient = dot(weighted_ref[...], kern_ref[...]) + dot_nt(mixed_ref[...], feats_ref[...])
    change = -STEP_SIZE * gradient
    base_ref[...] = change[:draws]
    for k, ref in enumerate(part_refs, 1):
        ref[...] = change[draws * k : draws * (k + 1)].astype(BF16)


def in_hbm(value):
    return pltpu.with_memory_space_constraint(value, pltpu.HBM)


def exchange(value):
    z, y = lax.axis_size("z"), lax.axis_size("y")
    order = [((ROOT[0] + a) % z) * y + (ROOT[1] + b) % y for a in range(z) for b in range(y)]
    groups = [[2 * chip + core for chip in order] for core in range(2)]
    return lax.all_to_all(value, POINT_AXES, 0, 0, axis_index_groups=groups)


def far_first(n_out):
    return sorted(range(1, n_out), key=lambda k: (-min(k, n_out - k), -k))


def swap_core(value):
    return lax.ppermute(value, "core", [(0, 1), (1, 0)])


def params(limit=None):
    return pltpu.CompilerParams(dimension_semantics=("arbitrary",), vmem_limit_bytes=limit)


def shards(points, rep_weights, batch_index, targets, noise_var, coregion, frequencies, phases):
    highest = lax.Precision.HIGHEST
    n_out = lax.axis_size("out")
    n_chips = lax.axis_size("z") * lax.axis_size("y")
    n_pts = 2 * n_chips
    rows, width = points.shape
    draws = rep_weights.shape[2]
    minibatch = batch_index.shape[0]
    own_rows = minibatch // n_out
    own_features = frequencies.shape[1] // n_out
    cols = n_out * draws
    out, core, chip = place_of_device()
    shard = chip * 2 + core
    ratio = (rows * n_pts) / minibatch

    own_weights = rep_weights[0].T
    low = own_weights.astype(BF16)
    weights = [low] * n_out
    for k in far_first(n_out):
        weights[k] = lax.ppermute(low, "out", [(i, (i - k) % n_out) for i in range(n_out)])
    weight_specs = lambda block: [pl.BlockSpec((draws, block), lambda i: (0, i))] * n_out
    point_spec = lambda block: pl.BlockSpec((block, width), lambda i: (i, 0))
    feat_spec = lambda block: pl.BlockSpec((block, own_features), lambda i: (i, 0))
    kern_spec = lambda block: pl.BlockSpec((own_rows, block), lambda i: (0, i))
    draw_spec = lambda block: pl.BlockSpec((draws, block), lambda i: (0, i))

    feats, held, sent_rows = pl.pallas_call(
        features_kernel,
        grid=(rows // FEATURES_BLOCK,),
        out_shape=(
            pltpu.HBM((rows, own_features), BF16),
            pltpu.VMEM((rows, own_features), BF16),
            jax.ShapeDtypeStruct((2 * SLOTS, width // 2), BF16),
        ),
        in_specs=[
            whole((1, minibatch)),
            point_spec(FEATURES_BLOCK),
            whole(frequencies.shape),
            whole((1, phases.shape[0])),
        ],
        out_specs=(
            feat_spec(FEATURES_BLOCK),
            pl.BlockSpec(memory_space=pltpu.VMEM),
            whole((2 * SLOTS, width // 2)),
        ),
        scratch_shapes=[pltpu.VMEM((2 * SLOTS, 128), jnp.int32), pltpu.VMEM((2 * SLOTS, width), F32)],
        compiler_params=params(SMALL_VMEM),
        name="features",
    )(in_hbm(batch_index[None]), in_hbm(points), in_hbm(frequencies), in_hbm(phases[None]))

    in_vmem = pl.BlockSpec(memory_space=pltpu.VMEM)
    pack = pl.pallas_call(
        functools.partial(project_kernel, n_out),
        out_shape=jax.ShapeDtypeStruct((n_chips, 32, 128), BF16),
        in_specs=[in_vmem] * (n_out + 2),
        out_specs=in_vmem,
        compiler_params=pltpu.CompilerParams(vmem_limit_bytes=SMALL_VMEM),
        name="project",
    )(*weights, pltpu.with_memory_space_constraint(held, pltpu.VMEM), sent_rows)
    got = exchange(pack)
    batch_index, points_now, targets, _ = lax.optimization_barrier((batch_index, points, targets, pack))

    key = batch_index * minibatch + lax.iota(jnp.int32, minibatch)
    rank = jnp.sum((key[None, :] < key[:, None]).astype(jnp.int32), 1)
    own_rank = lax.iota(jnp.int32, own_rows) * n_out + out
    chosen = own_rank[:, None] == rank[None, :]
    own_index = jnp.sum(jnp.where(chosen, batch_index[None, :], 0), 1)
    own_shard = own_index // rows
    starts = jnp.sum((own_index[None, :] < (own_shard * rows)[:, None]).astype(jnp.int32), 1)
    slot = lax.iota(jnp.int32, own_rows) - starts
    same_shard = (batch_index // rows)[None, :] == (batch_index // rows)[:, None]
    most = jnp.max(jnp.sum(same_shard.astype(jnp.int32), 1))
    overflow = most > SLOTS * n_out
    own_chip = own_shard // 2
    n_y = lax.axis_size("y")
    block = (own_chip // n_y - ROOT[0]) % lax.axis_size("z") * n_y + (own_chip - ROOT[1]) % n_y
    at = block * 32 + slot
    own_core = (own_shard % 2) == core
    at = jnp.stack([jnp.where(own_core, at, -64), jnp.where(own_core, -64, at)])
    at = jnp.broadcast_to(at[:, :, None], (2, own_rows, 128))
    col_norm = jnp.sum(jnp.square(points_now.astype(F32)), 1)[None]
    order = lax.rem(out + lax.iota(jnp.int32, n_out), n_out)
    own_targets = jnp.einsum("im,qms->qsi", chosen.astype(F32), targets, precision=highest)[order]
    own_targets = own_targets.reshape(cols, own_rows)
    got, at, overflow, own_index, col_norm, own_targets = lax.optimization_barrier(
        (got, at, overflow, own_index, col_norm, own_targets)
    )
    got_other = swap_core(got)

    def gram(direct, where):
        return pl.pallas_call(
            functools.partial(gram_kernel, n_out, direct),
            grid=(1,),
            out_shape=(
                jax.ShapeDtypeStruct((own_rows, rows), BF16),
                jax.ShapeDtypeStruct((cols // 2, own_rows), F32),
                jax.ShapeDtypeStruct((cols // 2, own_rows), F32),
                jax.ShapeDtypeStruct((8, 128), F32),
            ),
            in_specs=[pl.BlockSpec(memory_space=pltpu.VMEM)] * (n_out + 5),
            out_specs=(
                pl.BlockSpec(memory_space=pltpu.VMEM),
                pl.BlockSpec(memory_space=pltpu.VMEM),
                pl.BlockSpec(memory_space=pltpu.VMEM),
                pl.BlockSpec(memory_space=pltpu.VMEM),
            ),
            scratch_shapes=[
                pltpu.VMEM((own_rows, width), BF16),
                pltpu.VMEM((own_rows, 128), F32),
                pltpu.VMEM((cols, own_rows), F32),
            ],
            compiler_params=params(SMALL_VMEM),
            name="gram_fetched" if direct else "gram",
        )(*weights, where, got, got_other, pltpu.with_memory_space_constraint(points, pltpu.VMEM), col_norm)

    def fetch():
        local = own_index - shard * rows
        inside = (local >= 0) & (local < rows)
        picked = jnp.where(inside[:, None], points[jnp.clip(local, 0, rows - 1)].astype(F32), 0.0)
        return gram(True, lax.psum(picked, POINT_AXES).astype(BF16))

    kern, kept, given, tile = lax.cond(overflow, fetch, lambda: gram(False, at))

    pack = jnp.concatenate([kept + swap_core(given), tile], 0).astype(BF16)
    pack = jnp.broadcast_to(pack[None], (n_chips, *pack.shape))
    got = exchange(pack)
    got_other = swap_core(got)

    base, *parts = pl.pallas_call(
        functools.partial(step_kernel, n_out, ratio),
        grid=(rows // STEP_BLOCK,),
        out_shape=[jax.ShapeDtypeStruct((draws, rows), F32)]
        + [jax.ShapeDtypeStruct((draws, rows), BF16)] * (n_out - 1),
        in_specs=[
            pl.BlockSpec(memory_space=pltpu.SMEM),
            pl.BlockSpec(memory_space=pltpu.SMEM),
            whole(own_targets.shape),
            whole(got.shape),
            whole(got.shape),
            feat_spec(STEP_BLOCK),
            kern_spec(STEP_BLOCK),
        ],
        out_specs=[draw_spec(STEP_BLOCK)] * n_out,
        scratch_shapes=[pltpu.VMEM((cols, own_features), BF16), pltpu.VMEM((cols, own_rows), BF16)],
        compiler_params=params(SMALL_VMEM),
        name="step",
    )(coregion, noise_var, own_targets, got, got_other, in_hbm(feats), in_hbm(kern))
    total = own_weights + base
    for k in far_first(n_out):
        part = lax.ppermute(parts[k - 1], "out", [(i, (i + k) % n_out) for i in range(n_out)])
        total = total + part.astype(F32)
    return total.T[None]


def solution(mesh):
    fine = Mesh(mesh.devices.reshape(8, 4, 2, 4), ("z", "y", "core", "out"))
    in_specs = (P(POINT_AXES, None), P("out", POINT_AXES, None), P(), P(), P(), P(), P(), P())
    out_specs = P("out", POINT_AXES, None)
    return jax.shard_map(shards, mesh=fine, in_specs=in_specs, out_specs=out_specs, check_vma=False)
```
